128 devices in a mesh: phase: 4 (over y_lo, core), dp: 4 (over z), tensor: 8 (over x, y_hi).
Axes of the slice: x: 4, y: 4 (y_hi: 2, y_lo: 2; y = y_hi * 2 + y_lo), z: 4, core: 2. Of those that a mesh axis runs over, the one named last changes fastest.
Arguments:
- inputs: bfloat16 [4, 256, 8192], P(None, 'dp', 'tensor')
- seq_parts: int32 [4, 4, 6], P(None, 'dp'), may hold values from 1 to 32, 64 in all within a row
- norm_gain: float32 [4, 8192], P('phase'), may hold values from 0.4 to 2.5
- w_query: bfloat16 [4, 8192, 4096], P('phase', None, 'tensor')
- w_key: bfloat16 [4, 8192, 1024], P('phase', None, 'tensor')
- w_value: bfloat16 [4, 8192, 1024], P('phase', None, 'tensor'), may hold values from -0.0625 to 0.0625
- w_out: bfloat16 [4, 4096, 8192], P('phase', 'tensor'), may hold values from -0.375 to 0.375
Outputs:
- section_outputs: bfloat16 [4, 4, 256, 8192], P('phase', None, 'dp', 'tensor')
The draws below stay inside these ranges and needn't reach their ends.
Inputs may be any that keep to these rules, and one draw needn't show every extreme that they name: `seq_parts`: the entries of each data row sum to 64, and each data row's largest entry is exactly half of 64.
All inputs are finite; a program needn't handle non-finite values.
Results may differ from the reference program's by a relative error of at most 0.04.
Values may be sent and summed in bfloat16 or wider, within the bound.
No kernel may reach another device: no remote copies, remote signals or barrier semaphores. Data moves between devices by JAX's collectives and lax.ppermute only.
A program may use at most 128 MiB of HBM per device.

```python
import math
from functools import partial
import jax
import jax.numpy as jnp
import numpy as np
from jax import lax

D = 8192
HEADS = 32
KVH = 8
HD = 128
ROWS = 64
SEQS = 2
MICRO = 4
PHASES = 4
GROUPS = 8
DATA = 4
TOKENS = 256


def shared_keys(key):
    base = jnp.clip(jax.random.normal(key, (PHASES, D, KVH * HD), jnp.float32), -5.0, 5.0)
    return base * D ** (-0.5)


def draw_w_key(key, part):
    shared = shared_keys(key)
    return shared.astype(jnp.bfloat16)


def draw_w_query(key, part):
    key = jax.random.fold_in(key, 7)
    noise = jnp.clip(jax.random.normal(key, (PHASES, D, HEADS * HD), jnp.float32), -5.0, 5.0) * D ** (-0.5)
    return noise.astype(jnp.bfloat16)


def draw_inputs(key, part):
    key = jax.random.fold_in(key, 3)
    base_key, column_key, row_key = jax.random.split(key, 3)
    columns = jnp.arange(D, dtype=jnp.float32)
    column_scale = jnp.exp(columns * (math.log(3.0) / D)) * jnp.exp(jax.random.uniform(column_key, (D,), jnp.float32, math.log(0.5), math.log(1.5)))
    row_scale = jnp.exp(jax.random.uniform(row_key, (MICRO, TOKENS, 1), jnp.float32, math.log(0.4), math.log(4.0)))
    base = jnp.clip(jax.random.normal(base_key, (MICRO, TOKENS, D), jnp.float32), -4.0, 4.0)
    return jnp.clip(base * row_scale * column_scale[None, None, :], -64.0, 64.0).astype(jnp.bfloat16)


def with_spikes(drawn, own_key, source, target, parts, factor):
    def block_of(dim):
        return (jnp.arange(drawn.shape[dim]) // (drawn.shape[dim] // parts)).reshape((-1,) + (1,) * (drawn.ndim - 1 - dim))

    near = jax.random.permutation(own_key, parts)[block_of(target)]
    far = (block_of(target) + parts // 2) % parts
    return jnp.where((block_of(source) == near) | (block_of(source) == far), factor * drawn, drawn)


def shard_levels(stream_key, shape, cuts, least, top_value):
    gain = 1.0
    for axis_at, blocks in cuts:
        draws = jax.random.uniform(jax.random.fold_in(jax.random.fold_in(stream_key, 6), axis_at), (blocks,), jnp.float32, least / len(cuts), top_value / len(cuts))
        gain = gain * jnp.repeat(jnp.exp(draws), shape[axis_at] // blocks).reshape((-1,) + (1,) * (len(shape) - 1 - axis_at))
    return gain


def split_up(amount, total, limit, skew):
    weights = [(1 << 20) // math.isqrt(rank ** skew) + 1 for rank in range(2, amount + 1)]
    spare, holding = total - limit - (amount - 1), [1] * (amount - 1)
    while spare > 0:
        movable = [i for i in range(amount - 1) if holding[i] < limit]
        whole, left = sum([weights[i] for i in movable]), spare
        for i in movable:
            extra = min(limit - holding[i], max(1, left * weights[i] // whole), spare)
            holding[i] = holding[i] + extra
            spare = spare - extra
    return np.array([limit] + holding)


def ragged(rng, amount, total, bound, slope):
    if amount == 2:
        one = jax.random.randint(rng, (), max(1, total - bound), min(bound, total - 1) + 1)
        return jnp.stack([one, total - one])
    sizes = jnp.asarray(split_up(amount, total, bound, slope), jnp.int32)
    couples = (amount - 1) // 2
    giver, sink = sizes[1:1 + 2 * couples:2], sizes[2:2 + 2 * couples:2]
    slack = jnp.minimum(giver - 1, bound - sink)
    passed = jax.random.randint(jax.random.fold_in(rng, 1), (couples,), 0, 1 << 20) % (slack + 1)
    sizes = sizes.at[1:1 + 2 * couples:2].set(giver - passed).at[2:2 + 2 * couples:2].set(sink + passed)
    return sizes[jax.random.permutation(jax.random.fold_in(rng, 2), amount)]


def normal_values(rng, dims, spread, reach, cuts=(), held_as=jnp.bfloat16):
    result = jax.random.normal(rng, dims, jnp.float32) * spread
    if len(cuts) > 0:
        result = shard_levels(rng, dims, cuts, -0.22, 0.18) * result
    return jnp.clip(result, min=-reach, max=reach).astype(held_as)


def bell_draw_with(stream_key, shape, spread, reach, cuts, heavy, kind=jnp.bfloat16):
    drawn = spread * jax.random.normal(stream_key, shape, jnp.float32)
    if cuts:
        drawn = drawn * shard_levels(stream_key, shape, cuts, -0.22, 0.18)
    return jnp.clip(with_spikes(drawn, jax.random.fold_in(stream_key, 3), *heavy), -reach, reach).astype(kind)


def setup_inputs(seed: int = 0) -> dict:
    streams_of = jax.random.split(jax.random.key(seed), 8)
    inputs = draw_inputs(jax.random.fold_in(streams_of[7], 71), 0)
    seq_parts = jax.vmap(lambda own: ragged(own, 3 * SEQS, ROWS, ROWS // 2, 2))(jax.random.split(streams_of[1], MICRO * DATA)).reshape((MICRO, DATA, 3 * SEQS)).astype(jnp.int32)
    norm_gain = jnp.clip(jnp.exp(math.log(2.5) - 1.8325814 * jax.random.uniform(streams_of[2], (PHASES, D), jnp.float32) ** shard_levels(streams_of[2], (PHASES, D), ((0, 4),), -0.2, 0.2)), 0.4, 2.5)
    w_query = draw_w_query(jax.random.fold_in(streams_of[7], 71), 0)
    w_key = draw_w_key(jax.random.fold_in(streams_of[7], 71), 0)
    w_value = normal_values(streams_of[5], (PHASES, D, KVH * HD), D ** -0.5, 0.0625, ((0, 4), (2, 8)))
    w_out = bell_draw_with(streams_of[6], (PHASES, HEADS * HD, D), (HEADS * HD // 8) ** -0.5, 0.375, ((0, 4), (1, 8)), (1, 2, 8, 2.0))
    return dict(inputs=inputs, seq_parts=seq_parts, norm_gain=norm_gain, w_query=w_query, w_key=w_key, w_value=w_value, w_out=w_out)


epsilon = 1e-05
theta_base = 10000.0

def row_layout(part_lengths, row_count):
    lengths = lax.optimization_barrier(jnp.sum(part_lengths.reshape(-1, 3), axis=1)).astype(jnp.int32)
    seq_ends = jnp.cumsum(lengths).astype(jnp.int32)
    seq_starts = (seq_ends - lengths).astype(jnp.int32)
    places = jnp.arange(row_count, dtype=jnp.int32)
    segment = lax.optimization_barrier(jnp.sum((places[:, None] >= seq_ends[None, :]).astype(jnp.int32), axis=1)).astype(jnp.int32)
    owners = jnp.arange(lengths.shape[0], dtype=jnp.int32)
    seq_first = lax.optimization_barrier(jnp.sum(jnp.where(segment[:, None] == owners[None, :], seq_starts[None, :], 0), axis=1)).astype(jnp.int32)
    return (segment, (places - seq_first).astype(jnp.int32))

def rotate(projected, position):
    row_count = projected.shape[0]
    head_count = projected.shape[1] // HD
    half_size = HD // 2
    frequency = jnp.exp(jnp.arange(half_size, dtype=jnp.float32) * (-2.0 * math.log(theta_base) / HD))
    angles = position.astype(jnp.float32)[:, None] * frequency[None, :]
    cosine = jnp.cos(angles)[:, None, :]
    sine_part = jnp.sin(angles)[:, None, :]
    split_heads = projected.reshape(row_count, head_count, HD)
    first_half = split_heads[..., :half_size]
    second_half = split_heads[..., half_size:]
    turned = jnp.concatenate([first_half * cosine - second_half * sine_part, second_half * cosine + first_half * sine_part], axis=-1)
    return turned.reshape(row_count, head_count * HD)

def attend(queries, keys, values, segment, position):
    row_count = queries.shape[0]
    kv_heads = keys.shape[1] // HD
    group_size = queries.shape[1] // keys.shape[1]
    query_heads = queries.reshape(row_count, kv_heads, group_size, HD).astype(jnp.float32)
    key_heads = keys.reshape(row_count, kv_heads, HD).astype(jnp.float32)
    value_heads = values.reshape(row_count, kv_heads, HD).astype(jnp.float32)
    scores = jnp.einsum('qhgd,shd->hgqs', query_heads, key_heads) / math.sqrt(HD)
    allowed = (segment[:, None] == segment[None, :]) & (position[None, :] <= position[:, None])
    scores = jnp.where(allowed[None, None], scores, -1e+30)
    peak = lax.optimization_barrier(jnp.max(scores, axis=-1, keepdims=True))
    weights = jnp.exp(scores - peak)
    shares = (weights / lax.optimization_barrier(jnp.sum(weights, axis=-1, keepdims=True))).astype(jnp.bfloat16)
    mixed = jnp.einsum('hgqs,shd->qhgd', shares.astype(jnp.float32), value_heads)
    return mixed.reshape(row_count, -1).astype(jnp.bfloat16)

def section(current, gain_row, query_w, key_w, value_w, out_w, segment, position):
    wide_state = current.astype(jnp.float32)
    mean_square = lax.optimization_barrier(jnp.mean(wide_state * wide_state, axis=1, keepdims=True))
    normed = (wide_state * lax.rsqrt(mean_square + epsilon) * gain_row[None, :]).astype(jnp.bfloat16)
    queries = rotate(jnp.dot(normed, query_w, preferred_element_type=jnp.float32), position).astype(jnp.bfloat16)
    keys = rotate(jnp.dot(normed, key_w, preferred_element_type=jnp.float32), position).astype(jnp.bfloat16)
    values = jnp.dot(normed, value_w, preferred_element_type=jnp.float32).astype(jnp.bfloat16)
    token_count = current.shape[0]
    heads_out = jax.vmap(attend)(queries.reshape(DATA, ROWS, -1), keys.reshape(DATA, ROWS, -1), values.reshape(DATA, ROWS, -1), segment.reshape(DATA, ROWS), position.reshape(DATA, ROWS)).reshape(token_count, -1)
    share_width = heads_out.shape[1] // GROUPS
    head_total = jnp.zeros(current.shape, jnp.float32)
    for member in range(GROUPS):
        lower = member * share_width
        upper = lower + share_width
        partial_sum = jnp.dot(heads_out[:, lower:upper], out_w[lower:upper], preferred_element_type=jnp.float32)
        rounded = lax.optimization_barrier(partial_sum.astype(jnp.bfloat16))
        head_total = head_total + rounded.astype(jnp.float32)
    return (wide_state + head_total).astype(jnp.bfloat16)

def reference(inputs, seq_parts, norm_gain, w_query, w_key, w_value, w_out):
    outputs = []
    for micro_index in range(MICRO):
        segment, position = jax.vmap(partial(row_layout, row_count=ROWS))(seq_parts[micro_index])
        segment = segment.reshape(-1)
        position = position.reshape(-1)
        current = inputs[micro_index]
        per_phase = []
        for phase_index in range(PHASES):
            current = section(current, norm_gain[phase_index], w_query[phase_index], w_key[phase_index], w_value[phase_index], w_out[phase_index], segment, position)
            per_phase.append(current)
        outputs.append(jnp.stack(per_phase))
    return jnp.stack(outputs, axis=1)
```

```python
import math

import jax
import jax.numpy as jnp
from jax import lax
from jax.experimental import pallas as pl
from jax.experimental.pallas import tpu as pltpu
from jax.sharding import PartitionSpec as P

D = 8192
HD = 128
QF = 512
KF = 128
ROWS = 64
CHUNK = 1024
MICRO = 4
PEERS = 8
epsilon = 1e-05
theta_base = 10000.0

OFFSETS = [(2, 1), (2, 0), (1, 1), (3, 1), (1, 0), (3, 0), (0, 1), (0, 0)]


def moved(place, offset):
    x, y = place // 2, place % 2
    return ((x + offset[0]) % 4) * 2 + (y + offset[1]) % 2


def shift(value, offset, from_phase, to_phase):
    pairs = [(from_phase * PEERS + t, to_phase * PEERS + moved(t, offset)) for t in range(PEERS)]
    return lax.ppermute(value, ("phase", "tensor"), pairs)


def heads_kernel(
    source_ref, first_ref, cos_ref, sin_ref, gain_ref, *refs
):
    chunks = refs[:PEERS]
    query_hbm, key_hbm, value_hbm, out_ref = refs[PEERS:PEERS + 4]
    query_w, key_w, value_w, total, squares, copied = refs[PEERS + 4:]
    rows = out_ref.shape[0]

    def copies(j):
        begin = pl.multiple_of(source_ref[j] * CHUNK, CHUNK)
        held = pl.ds(j * CHUNK, CHUNK)
        return [
            pltpu.make_async_copy(query_hbm.at[pl.ds(begin, CHUNK)], query_w.at[held], copied.at[j, 0]),
            pltpu.make_async_copy(key_hbm.at[pl.ds(begin, CHUNK)], key_w.at[held], copied.at[j, 1]),
            pltpu.make_async_copy(value_hbm.at[pl.ds(begin, CHUNK)], value_w.at[held], copied.at[j, 2]),
        ]

    for j in range(PEERS):
        for copy in copies(j):
            copy.start()
    for j in range(PEERS):
        wide = chunks[j][...].astype(jnp.float32)
        gain = gain_ref[pl.ds(source_ref[j], 1), :]
        scaled = (wide * gain).astype(jnp.bfloat16)
        square = jnp.sum(wide * wide, axis=1, keepdims=True)
        for copy in copies(j):
            copy.wait()
        held = slice(j * CHUNK, (j + 1) * CHUNK)
        parts = [
            (slice(0, QF), query_w), (slice(QF, QF + KF), key_w), (slice(QF + KF, QF + 2 * KF), value_w)
        ]
        for columns, weight in parts:
            term = jnp.dot(scaled, weight[held, :], preferred_element_type=jnp.float32)
            if j == 0:
                total[:, columns] = term
            else:
                total[:, columns] += term
        if j == 0:
            squares[...] = square
        else:
            squares[...] += square
    scale = lax.rsqrt(squares[...] / D + epsilon)
    cosine = cos_ref[...]
    sine = sin_ref[...]

    def turned(part):
        part = part * scale
        return (part * cosine + pltpu.roll(part, HD // 2, 1) * sine).astype(jnp.bfloat16)

    queries = [turned(total[:, i * HD:(i + 1) * HD]) for i in range(QF // HD)]
    keys = turned(total[:, QF:QF + KF])
    values = (total[:, QF + KF:] * scale).astype(jnp.bfloat16)
    heads = QF // HD
    row = lax.broadcasted_iota(jnp.int32, (heads * ROWS, ROWS), 0) % ROWS
    column = lax.broadcasted_iota(jnp.int32, (heads * ROWS, ROWS), 1)
    for m in range(rows // ROWS):
        own = slice(m * ROWS, (m + 1) * ROWS)
        first = first_ref[m]
        query = jnp.concatenate([q[own] for q in queries], axis=0)
        scores = lax.dot_general(
            query, keys[own], (((1,), (1,)), ((), ())), preferred_element_type=jnp.float32
        ) / math.sqrt(HD)
        allowed = (column <= row) & ((row < first) | (column >= first))
        scores = jnp.where(allowed, scores, -1e30)
        weights = jnp.exp(scores - jnp.max(scores, axis=1, keepdims=True))
        shares = (weights / jnp.sum(weights, axis=1, keepdims=True)).astype(jnp.bfloat16)
        mixed = jnp.dot(shares, values[own], preferred_element_type=jnp.float32).astype(jnp.bfloat16)
        for i in range(heads):
            out_ref[own, i * HD:(i + 1) * HD] = mixed[i * ROWS:(i + 1) * ROWS]


def heads_call(source, first, cosine, sine, gain, chunks, query_w, key_w, value_w):
    rows = chunks[0].shape[0]
    vmem = pl.BlockSpec(memory_space=pltpu.VMEM)
    smem = pl.BlockSpec(memory_space=pltpu.SMEM)
    hbm = pl.BlockSpec(memory_space=pl.ANY)
    return pl.pallas_call(
        heads_kernel,
        out_shape=jax.ShapeDtypeStruct((rows, QF), jnp.bfloat16),
        in_specs=[smem, smem, vmem, vmem, vmem] + [vmem] * PEERS + [hbm] * 3,
        out_specs=vmem,
        scratch_shapes=[
            pltpu.VMEM((D, QF), jnp.bfloat16),
            pltpu.VMEM((D, KF), jnp.bfloat16),
            pltpu.VMEM((D, KF), jnp.bfloat16),
            pltpu.VMEM((rows, QF + 2 * KF), jnp.float32),
            pltpu.VMEM((rows, 1), jnp.float32),
            pltpu.SemaphoreType.DMA((PEERS, 3)),
        ],
        compiler_params=pltpu.CompilerParams(vmem_limit_bytes=40 * 2**20),
        cost_estimate=pl.CostEstimate(
            flops=2 * rows * D * (QF + 2 * KF), bytes_accessed=2 * D * (QF + 2 * KF), transcendentals=0
        ),
        name="heads",
    )(source, first, cosine, sine, gain, *chunks, query_w, key_w, value_w)


def terms_kernel(target_ref, heads_ref, weight_hbm, *refs):
    count = len(refs) - 2
    outs, weight, copied = refs[:count], refs[count], refs[count + 1]

    def copy(j):
        begin = pl.multiple_of(target_ref[j] * CHUNK, CHUNK)
        return pltpu.make_async_copy(
            weight_hbm.at[:, pl.ds(begin, CHUNK)], weight.at[j], copied.at[j]
        )

    for j in range(count):
        copy(j).start()
    for j in range(count):
        copy(j).wait()
        outs[j][...] = jnp.dot(
            heads_ref[...], weight[j], preferred_element_type=jnp.float32
        ).astype(jnp.bfloat16)


def terms_call(target, heads_out, weight):
    rows = heads_out.shape[0]
    count = target.shape[0]
    vmem = pl.BlockSpec(memory_space=pltpu.VMEM)
    return pl.pallas_call(
        terms_kernel,
        out_shape=[jax.ShapeDtypeStruct((rows, CHUNK), jnp.bfloat16)] * count,
        in_specs=[pl.BlockSpec(memory_space=pltpu.SMEM), vmem, pl.BlockSpec(memory_space=pl.ANY)],
        out_specs=[vmem] * count,
        scratch_shapes=[
            pltpu.VMEM((count, QF, CHUNK), jnp.bfloat16),
            pltpu.SemaphoreType.DMA((count,)),
        ],
        compiler_params=pltpu.CompilerParams(vmem_limit_bytes=24 * 2**20),
        cost_estimate=pl.CostEstimate(
            flops=2 * rows * QF * CHUNK * count, bytes_accessed=2 * QF * CHUNK * count, transcendentals=0
        ),
        name="terms",
    )(target, heads_out, weight)


def places(seq_parts):
    first = jnp.sum(seq_parts[:, 0, :3], axis=1)
    row = jnp.arange(ROWS, dtype=jnp.int32)[None, :]
    position = jnp.where(row < first[:, None], row, row - first[:, None]).reshape(-1)
    half = HD // 2
    frequency = jnp.exp(
        jnp.arange(half, dtype=jnp.float32) * (-2.0 * math.log(theta_base) / HD)
    )
    angles = position.astype(jnp.float32)[:, None] * frequency[None, :]
    cosine, sine = jnp.cos(angles), jnp.sin(angles)
    return (
        first,
        jnp.concatenate([cosine, cosine], axis=1),
        jnp.concatenate([-sine, sine], axis=1),
    )


def on_device(inputs, seq_parts, norm_gain, w_query, w_key, w_value, w_out):
    phase_count = lax.axis_size("phase")
    phase_index = lax.axis_index("phase")
    me = lax.axis_index("tensor")
    x, y = me // 2, me % 2
    source = jnp.stack([((x - dx) % 4) * 2 + (y - dy) % 2 for dx, dy in OFFSETS]).astype(jnp.int32)
    target = jnp.stack([((x + dx) % 4) * 2 + (y + dy) % 2 for dx, dy in OFFSETS]).astype(jnp.int32)
    first, cosine, sine = places(seq_parts)
    gain = norm_gain.reshape(PEERS, CHUNK)
    own = inputs.reshape(MICRO * ROWS, CHUNK)
    result = jnp.zeros_like(own)
    for phase in range(phase_count):
        if phase == 0:
            chunks = [shift(own, offset, 0, 0) for offset in OFFSETS[:-1]] + [own]
        else:
            chunks = [shift(own, offset, phase - 1, phase) for offset in OFFSETS]
        heads_out = heads_call(
            source, first, cosine, sine, gain, chunks, w_query[0], w_key[0], w_value[0]
        )
        terms = terms_call(target, heads_out, w_out[0])
        arrived = [shift(term, offset, phase, phase) for term, offset in zip(terms[:-1], OFFSETS[:-1])]
        head_total = terms[-1].astype(jnp.float32)
        for term in arrived:
            head_total = head_total + term.astype(jnp.float32)
        own = (chunks[-1].astype(jnp.float32) + head_total).astype(jnp.bfloat16)
        result = jnp.where(phase_index == phase, own, result)
    return result.reshape(1, MICRO, ROWS, CHUNK)


def solution(mesh):
    placed = (
        P(None, "dp", "tensor"),
        P(None, "dp", None),
        P("phase", None),
        P("phase", None, "tensor"),
        P("phase", None, "tensor"),
        P("phase", None, "tensor"),
        P("phase", "tensor", None),
    )
    return jax.shard_map(
        on_device,
        mesh=mesh,
        in_specs=placed,
        out_specs=P("phase", None, "dp", "tensor"),
        check_vma=False,
    )
```

```python
import math

import jax
import jax.numpy as jnp
from jax import lax
from jax.experimental import pallas as pl
from jax.experimental.pallas import tpu as pltpu
from jax.sharding import PartitionSpec as P

D = 8192
HD = 128
QF = 512
KF = 128
ROWS = 64
CHUNK = 1024
MICRO = 4
PEERS = 8
epsilon = 1e-05
theta_base = 10000.0

STEPS = (2, 1, 3, 0)


def along_x(value, step, hops):
    pairs = [
        (start * PEERS + x * 2 + y, end * PEERS + ((x + step) % 4) * 2 + y)
        for start, end in hops for x in range(4) for y in range(2)
    ]
    return lax.ppermute(value, ("phase", "tensor"), pairs)


def along_y(value, phases):
    pairs = [(phase * PEERS + t, phase * PEERS + (t ^ 1)) for phase in phases for t in range(PEERS)]
    return lax.ppermute(value, ("phase", "tensor"), pairs)


def add_products(source_ref, gain_ref, chunks, weights, total, squares, fresh):
    for j, chunk in enumerate(chunks):
        wide = chunk[...].astype(jnp.float32)
        gain = gain_ref[pl.ds(source_ref[j], 1), :]
        scaled = (wide * gain).astype(jnp.bfloat16)
        square = jnp.sum(wide * wide, axis=1, keepdims=True)
        held = pl.ds(pl.multiple_of(source_ref[j] * CHUNK, CHUNK), CHUNK)
        begin = 0
        for weight in weights:
            columns = slice(begin, begin + weight.shape[1])
            begin = columns.stop
            term = jnp.dot(scaled, weight[held, :], preferred_element_type=jnp.float32)
            if fresh and j == 0:
                total[:, columns] = term
            else:
                total[:, columns] += term
        if fresh and j == 0:
            squares[...] = jnp.broadcast_to(square, squares.shape)
        else:
            squares[...] += square


def first_kernel(source_ref, gain_ref, *refs):
    count = len(refs) - 5
    chunks, weights, total, squares = refs[:count], refs[count:count + 3], refs[-2], refs[-1]
    add_products(source_ref, gain_ref, chunks, weights, total, squares, True)


def heads_kernel(source_ref, first_ref, gain_ref, cos_ref, sin_ref, begun_ref, squares_ref, *refs):
    count = len(refs) - 6
    chunks, weights, out_ref, total, squares = (
        refs[:count], refs[count:count + 3], refs[-3], refs[-2], refs[-1]
    )
    rows = out_ref.shape[0]
    total[...] = begun_ref[...]
    squares[...] = squares_ref[...]
    add_products(source_ref, gain_ref, chunks, weights, total, squares, False)
    scale = lax.rsqrt(squares[...] / D + epsilon)
    cosine = cos_ref[...]
    sine = sin_ref[...]

    def turned(part):
        part = part * scale
        return (part * cosine + pltpu.roll(part, HD // 2, 1) * sine).astype(jnp.bfloat16)

    queries = [turned(total[:, i * HD:(i + 1) * HD]) for i in range(QF // HD)]
    keys = turned(total[:, QF:QF + KF])
    values = (total[:, QF + KF:] * scale).astype(jnp.bfloat16)
    heads = QF // HD
    row = lax.broadcasted_iota(jnp.int32, (heads * ROWS, ROWS), 0) % ROWS
    column = lax.broadcasted_iota(jnp.int32, (heads * ROWS, ROWS), 1)
    for m in range(rows // ROWS):
        own = slice(m * ROWS, (m + 1) * ROWS)
        first = first_ref[m]
        query = jnp.concatenate([q[own] for q in queries], axis=0)
        scores = lax.dot_general(
            query, keys[own], (((1,), (1,)), ((), ())), preferred_element_type=jnp.float32
        ) / math.sqrt(HD)
        allowed = (column <= row) & ((row < first) | (column >= first))
        scores = jnp.where(allowed, scores, -1e30)
        weights_of = jnp.exp(scores - jnp.max(scores, axis=1, keepdims=True))
        shares = (weights_of / jnp.sum(weights_of, axis=1, keepdims=True)).astype(jnp.bfloat16)
        mixed = jnp.dot(shares, values[own], preferred_element_type=jnp.float32).astype(jnp.bfloat16)
        for i in range(heads):
            out_ref[own, i * HD:(i + 1) * HD] = mixed[i * ROWS:(i + 1) * ROWS]


VMEM = pl.BlockSpec(memory_space=pltpu.VMEM)
SMEM = pl.BlockSpec(memory_space=pltpu.SMEM)
WIDE = QF + 2 * KF


def first_call(source, gain, chunks, weights):
    rows = chunks[0].shape[0]
    return pl.pallas_call(
        first_kernel,
        out_shape=[
            jax.ShapeDtypeStruct((rows, WIDE), jnp.float32),
            jax.ShapeDtypeStruct((rows, HD), jnp.float32),
        ],
        in_specs=[SMEM] + [VMEM] * (1 + len(chunks) + 3),
        out_specs=[VMEM] * 2,
        compiler_params=pltpu.CompilerParams(vmem_limit_bytes=8 * 2**20),
        cost_estimate=pl.CostEstimate(
            flops=2 * rows * len(chunks) * CHUNK * WIDE,
            bytes_accessed=2 * len(chunks) * CHUNK * WIDE, transcendentals=0
        ),
        name="first",
    )(source, gain, *chunks, *weights)


def heads_call(source, first, gain, cosine, sine, begun, squares, chunks, weights):
    rows = chunks[0].shape[0]
    return pl.pallas_call(
        heads_kernel,
        out_shape=jax.ShapeDtypeStruct((rows, QF), jnp.bfloat16),
        in_specs=[SMEM, SMEM] + [VMEM] * (5 + len(chunks) + 3),
        out_specs=VMEM,
        scratch_shapes=[
            pltpu.VMEM((rows, WIDE), jnp.float32),
            pltpu.VMEM((rows, HD), jnp.float32),
        ],
        compiler_params=pltpu.CompilerParams(vmem_limit_bytes=8 * 2**20),
        cost_estimate=pl.CostEstimate(
            flops=2 * rows * len(chunks) * CHUNK * WIDE,
            bytes_accessed=2 * len(chunks) * CHUNK * WIDE, transcendentals=0
        ),
        name="heads",
    )(source, first, gain, cosine, sine, begun, squares, *chunks, *weights)


def terms_kernel(target_ref, heads_ref, weight, *outs):
    for j, out in enumerate(outs):
        held = pl.ds(pl.multiple_of(target_ref[j] * CHUNK, CHUNK), CHUNK)
        out[...] = jnp.dot(
            heads_ref[...], weight[:, held], preferred_element_type=jnp.float32
        ).astype(jnp.bfloat16)


def terms_call(target, heads_out, weight):
    rows = heads_out.shape[0]
    count = target.shape[0]
    return pl.pallas_call(
        terms_kernel,
        out_shape=[jax.ShapeDtypeStruct((rows, CHUNK), jnp.bfloat16)] * count,
        in_specs=[SMEM, VMEM, VMEM],
        out_specs=[VMEM] * count,
        compiler_params=pltpu.CompilerParams(vmem_limit_bytes=8 * 2**20),
        cost_estimate=pl.CostEstimate(
            flops=2 * rows * QF * CHUNK * count, bytes_accessed=2 * QF * CHUNK * count, transcendentals=0
        ),
        name="terms",
    )(target, heads_out, weight)


def places(seq_parts):
    first = jnp.sum(seq_parts[:, 0, :3], axis=1)
    row = jnp.arange(ROWS, dtype=jnp.int32)[None, :]
    position = jnp.where(row < first[:, None], row, row - first[:, None]).reshape(-1)
    half = HD // 2
    frequency = jnp.exp(
        jnp.arange(half, dtype=jnp.float32) * (-2.0 * math.log(theta_base) / HD)
    )
    angles = position.astype(jnp.float32)[:, None] * frequency[None, :]
    cosine, sine = jnp.cos(angles), jnp.sin(angles)
    return (
        first,
        jnp.concatenate([cosine, cosine], axis=1),
        jnp.concatenate([-sine, sine], axis=1),
    )


def plus(one, other):
    return (one.astype(jnp.float32) + other.astype(jnp.float32)).astype(jnp.bfloat16)


def on_device(inputs, seq_parts, norm_gain, w_query, w_key, w_value, w_out):
    phase_count = lax.axis_size("phase")
    phase_index = lax.axis_index("phase")
    me = lax.axis_index("tensor")
    x, y = me // 2, me % 2
    near_source = jnp.stack([((x - step) % 4) * 2 + y for step in STEPS]).astype(jnp.int32)
    near_target = jnp.stack([((x + step) % 4) * 2 + y for step in STEPS]).astype(jnp.int32)
    far_source, far_target = near_source ^ 1, near_target ^ 1
    first, cosine, sine = places(seq_parts)
    gain = norm_gain.reshape(PEERS, CHUNK)
    weights = (w_query[0], w_key[0], w_value[0])
    own = inputs.reshape(MICRO * ROWS, CHUNK)
    result = jnp.zeros_like(own)
    for phase in range(phase_count):
        alike = [p for p in range(phase_count) if p % 2 == phase % 2]
        stay = [(p, p) for p in alike]
        if phase == 0:
            near = [along_x(own, step, stay) for step in STEPS[:-1]] + [own]
        else:
            near = [along_x(own, step, [(phase - 1, phase)]) for step in STEPS]
        far = [along_y(chunk, alike) for chunk in near]
        begun, squares = first_call(near_source, gain, near, weights)
        heads_out = heads_call(
            far_source, first, gain, cosine, sine, begun, squares, far, weights
        )
        far_terms = terms_call(far_target, heads_out, w_out[0])
        arrived = [along_y(term, alike) for term in far_terms]
        near_terms = terms_call(near_target, heads_out, w_out[0])
        sums = [plus(term, other) for term, other in zip(near_terms, arrived)]
        total = near[-1].astype(jnp.float32) + sums[-1].astype(jnp.float32)
        for part, step in zip(sums[:-1], STEPS[:-1]):
            total = total + along_x(part, step, stay).astype(jnp.float32)
        own = total.astype(jnp.bfloat16)
        result = jnp.where(phase_index == phase, own, result)
    return result.reshape(1, MICRO, ROWS, CHUNK)


def solution(mesh):
    placed = (
        P(None, "dp", "tensor"),
        P(None, "dp", None),
        P("phase", None),
        P("phase", None, "tensor"),
        P("phase", None, "tensor"),
        P("phase", None, "tensor"),
        P("phase", "tensor", None),
    )
    return jax.shard_map(
        on_device,
        mesh=mesh,
        in_specs=placed,
        out_specs=P("phase", None, "dp", "tensor"),
        check_vma=False,
    )
```

```python
import math

import jax
import jax.numpy as jnp
from jax import lax
from jax.experimental import pallas as pl
from jax.experimental.pallas import tpu as pltpu
from jax.sharding import PartitionSpec as P

D = 8192
HD = 128
QF = 512
KF = 128
ROWS = 64
CHUNK = 1024
MICRO = 4
GROUPS = 2
PEERS = 8
epsilon = 1e-05
theta_base = 10000.0

STEPS = (2, 1, 3, 0)


def along_x(value, step, hops):
    pairs = [
        (start * PEERS + x * 2 + y, end * PEERS + ((x + step) % 4) * 2 + y)
        for start, end in hops for x in range(4) for y in range(2)
    ]
    return lax.ppermute(value, ("phase", "tensor"), pairs)


def along_y(value, phases):
    pairs = [(phase * PEERS + t, phase * PEERS + (t ^ 1)) for phase in phases for t in range(PEERS)]
    return lax.ppermute(value, ("phase", "tensor"), pairs)


def add_products(source_ref, gain_ref, chunks, weights, total, squares, fresh):
    for j, chunk in enumerate(chunks):
        wide = chunk[...].astype(jnp.float32)
        gain = gain_ref[pl.ds(source_ref[j], 1), :]
        scaled = (wide * gain).astype(jnp.bfloat16)
        square = jnp.sum(wide * wide, axis=1, keepdims=True)
        held = pl.ds(pl.multiple_of(source_ref[j] * CHUNK, CHUNK), CHUNK)
        begin = 0
        for weight in weights:
            columns = slice(begin, begin + weight.shape[1])
            begin = columns.stop
            term = jnp.dot(scaled, weight[held, :], preferred_element_type=jnp.float32)
            if fresh and j == 0:
                total[:, columns] = term
            else:
                total[:, columns] += term
        if fresh and j == 0:
            squares[...] = jnp.broadcast_to(square, squares.shape)
        else:
            squares[...] += square


def first_kernel(source_ref, gain_ref, *refs):
    count = len(refs) - 5
    chunks, weights, total, squares = refs[:count], refs[count:count + 3], refs[-2], refs[-1]
    add_products(source_ref, gain_ref, chunks, weights, total, squares, True)


def heads_kernel(source_ref, first_ref, group_ref, gain_ref, cos_ref, sin_ref, begun_ref, squares_ref, *refs):
    count = len(refs) - 6
    chunks, weights, out_ref, total, squares = (
        refs[:count], refs[count:count + 3], refs[-3], refs[-2], refs[-1]
    )
    rows = out_ref.shape[0]
    total[...] = begun_ref[...]
    squares[...] = squares_ref[...]
    add_products(source_ref, gain_ref, chunks, weights, total, squares, False)
    scale = lax.rsqrt(squares[...] / D + epsilon)
    group = group_ref[0]
    placed = pl.ds(pl.multiple_of(group * rows, rows), rows)
    cosine = cos_ref[placed, :]
    sine = sin_ref[placed, :]

    def turned(part):
        part = part * scale
        return (part * cosine + pltpu.roll(part, HD // 2, 1) * sine).astype(jnp.bfloat16)

    queries = [turned(total[:, i * HD:(i + 1) * HD]) for i in range(QF // HD)]
    keys = turned(total[:, QF:QF + KF])
    values = (total[:, QF + KF:] * scale).astype(jnp.bfloat16)
    heads = QF // HD
    row = lax.broadcasted_iota(jnp.int32, (heads * ROWS, ROWS), 0) % ROWS
    column = lax.broadcasted_iota(jnp.int32, (heads * ROWS, ROWS), 1)
    for m in range(rows // ROWS):
        own = slice(m * ROWS, (m + 1) * ROWS)
        first = first_ref[group * (rows // ROWS) + m]
        query = jnp.concatenate([q[own] for q in queries], axis=0)
        scores = lax.dot_general(
            query, keys[own], (((1,), (1,)), ((), ())), preferred_element_type=jnp.float32
        ) / math.sqrt(HD)
        allowed = (column <= row) & ((row < first) | (column >= first))
        scores = jnp.where(allowed, scores, -1e30)
        weights_of = jnp.exp(scores - jnp.max(scores, axis=1, keepdims=True))
        shares = (weights_of / jnp.sum(weights_of, axis=1, keepdims=True)).astype(jnp.bfloat16)
        mixed = jnp.dot(shares, values[own], preferred_element_type=jnp.float32).astype(jnp.bfloat16)
        for i in range(heads):
            out_ref[own, i * HD:(i + 1) * HD] = mixed[i * ROWS:(i + 1) * ROWS]


VMEM = pl.BlockSpec(memory_space=pltpu.VMEM)
SMEM = pl.BlockSpec(memory_space=pltpu.SMEM)
WIDE = QF + 2 * KF


def first_call(source, gain, chunks, weights):
    rows = chunks[0].shape[0]
    return pl.pallas_call(
        first_kernel,
        out_shape=[
            jax.ShapeDtypeStruct((rows, WIDE), jnp.float32),
            jax.ShapeDtypeStruct((rows, HD), jnp.float32),
        ],
        in_specs=[SMEM] + [VMEM] * (1 + len(chunks) + 3),
        out_specs=[VMEM] * 2,
        compiler_params=pltpu.CompilerParams(vmem_limit_bytes=8 * 2**20),
        cost_estimate=pl.CostEstimate(
            flops=2 * rows * len(chunks) * CHUNK * WIDE,
            bytes_accessed=2 * len(chunks) * CHUNK * WIDE, transcendentals=0
        ),
        name="first",
    )(source, gain, *chunks, *weights)


def heads_call(source, first, group, gain, cosine, sine, begun, squares, chunks, weights):
    rows = chunks[0].shape[0]
    return pl.pallas_call(
        heads_kernel,
        out_shape=jax.ShapeDtypeStruct((rows, QF), jnp.bfloat16),
        in_specs=[SMEM, SMEM, SMEM] + [VMEM] * (5 + len(chunks) + 3),
        out_specs=VMEM,
        scratch_shapes=[
            pltpu.VMEM((rows, WIDE), jnp.float32),
            pltpu.VMEM((rows, HD), jnp.float32),
        ],
        compiler_params=pltpu.CompilerParams(vmem_limit_bytes=8 * 2**20),
        cost_estimate=pl.CostEstimate(
            flops=2 * rows * len(chunks) * CHUNK * WIDE,
            bytes_accessed=2 * len(chunks) * CHUNK * WIDE, transcendentals=0
        ),
        name="heads",
    )(source, first, group, gain, cosine, sine, begun, squares, *chunks, *weights)


def terms_kernel(target_ref, heads_ref, weight, *outs):
    for j, out in enumerate(outs):
        held = pl.ds(pl.multiple_of(target_ref[j] * CHUNK, CHUNK), CHUNK)
        out[...] = jnp.dot(
            heads_ref[...], weight[:, held], preferred_element_type=jnp.float32
        ).astype(jnp.bfloat16)


def terms_call(target, heads_out, weight):
    rows = heads_out.shape[0]
    count = target.shape[0]
    return pl.pallas_call(
        terms_kernel,
        out_shape=[jax.ShapeDtypeStruct((rows, CHUNK), jnp.bfloat16)] * count,
        in_specs=[SMEM, VMEM, VMEM],
        out_specs=[VMEM] * count,
        compiler_params=pltpu.CompilerParams(vmem_limit_bytes=8 * 2**20),
        cost_estimate=pl.CostEstimate(
            flops=2 * rows * QF * CHUNK * count, bytes_accessed=2 * QF * CHUNK * count, transcendentals=0
        ),
        name="terms",
    )(target, heads_out, weight)


def places(seq_parts):
    first = jnp.sum(seq_parts[:, 0, :3], axis=1)
    row = jnp.arange(ROWS, dtype=jnp.int32)[None, :]
    position = jnp.where(row < first[:, None], row, row - first[:, None]).reshape(-1)
    half = HD // 2
    frequency = jnp.exp(
        jnp.arange(half, dtype=jnp.float32) * (-2.0 * math.log(theta_base) / HD)
    )
    angles = position.astype(jnp.float32)[:, None] * frequency[None, :]
    cosine, sine = jnp.cos(angles), jnp.sin(angles)
    return (
        first,
        jnp.concatenate([cosine, cosine], axis=1),
        jnp.concatenate([-sine, sine], axis=1),
    )


def plus(one, other):
    return (one.astype(jnp.float32) + other.astype(jnp.float32)).astype(jnp.bfloat16)


def on_device(inputs, seq_parts, norm_gain, w_query, w_key, w_value, w_out):
    phase_count = lax.axis_size("phase")
    phase_index = lax.axis_index("phase")
    me = lax.axis_index("tensor")
    x, y = me // 2, me % 2
    near_source = jnp.stack([((x - step) % 4) * 2 + y for step in STEPS]).astype(jnp.int32)
    near_target = jnp.stack([((x + step) % 4) * 2 + y for step in STEPS]).astype(jnp.int32)
    far_source, far_target = near_source ^ 1, near_target ^ 1
    first, cosine, sine = places(seq_parts)
    gain = norm_gain.reshape(PEERS, CHUNK)
    weights = (w_query[0], w_key[0], w_value[0])
    entering = inputs.reshape(GROUPS, MICRO * ROWS // GROUPS, CHUNK)
    results = [None] * GROUPS
    own = None
    for tick in range(phase_count + GROUPS - 1):
        low = min(max(tick - 1, 0), phase_count - 2)
        alike = [low, low + 1]
        stay = [(p, p) for p in alike]
        below = min(max(tick - 2, 0), phase_count - 3)
        hops = [(p, p + 1) for p in (below, below + 1)]
        if tick > 0:
            near = [along_x(own, step, hops) for step in STEPS]
        if tick < GROUPS:
            fresh = entering[tick]
            if tick > 0:
                fresh, _ = lax.optimization_barrier((fresh, own))
            gathered = [along_x(fresh, step, [(0, 0)]) for step in STEPS[:-1]] + [fresh]
            if tick > 0:
                near = [jnp.where(phase_index == 0, a, b) for a, b in zip(gathered, near)]
            else:
                near = gathered
        far = [along_y(chunk, alike) for chunk in near]
        group = jnp.clip(tick - phase_index, 0, GROUPS - 1).astype(jnp.int32).reshape(1)
        begun, squares = first_call(near_source, gain, near, weights)
        heads_out = heads_call(
            far_source, first, group, gain, cosine, sine, begun, squares, far, weights
        )
        far_terms = terms_call(far_target, heads_out, w_out[0])
        arrived = [along_y(term, alike) for term in far_terms]
        near_terms = terms_call(near_target, heads_out, w_out[0])
        sums = [plus(term, other) for term, other in zip(near_terms, arrived)]
        total = near[-1].astype(jnp.float32) + sums[-1].astype(jnp.float32)
        for part, step in zip(sums[:-1], STEPS[:-1]):
            total = total + along_x(part, step, stay).astype(jnp.float32)
        own = total.astype(jnp.bfloat16)
        for g in range(GROUPS):
            if tick == g:
                results[g] = own
            elif 0 <= tick - g < phase_count:
                results[g] = jnp.where(phase_index == tick - g, own, results[g])
        if tick + 1 < phase_count + GROUPS - 1:
            own, *kept = lax.optimization_barrier((own, *[r for r in results if r is not None]))
            results = kept + results[len(kept):]
    return jnp.concatenate(results, axis=0).reshape(1, MICRO, ROWS, CHUNK)


def solution(mesh):
    placed = (
        P(None, "dp", "tensor"),
        P(None, "dp", None),
        P("phase", None),
        P("phase", None, "tensor"),
        P("phase", None, "tensor"),
        P("phase", None, "tensor"),
        P("phase", "tensor", None),
    )
    return jax.shard_map(
        on_device,
        mesh=mesh,
        in_specs=placed,
        out_specs=P("phase", None, "dp", "tensor"),
        check_vma=False,
    )
```

```python
import math

import jax
import jax.numpy as jnp
from jax import lax
from jax.experimental import pallas as pl
from jax.experimental.pallas import tpu as pltpu
from jax.sharding import PartitionSpec as P

D = 8192
HD = 128
QF = 512
KF = 128
ROWS = 64
CHUNK = 1024
MICRO = 4
PEERS = 8
epsilon = 1e-05
theta_base = 10000.0

GATHERED = (0, 1, 3, 2)
REDUCED = (2, 1, 3, 0)


def moved(value, step, cross, hops):
    pairs = [
        (start * PEERS + x * 2 + y, end * PEERS + ((x + step) % 4) * 2 + (y ^ cross))
        for start, end in hops for x in range(4) for y in range(2)
    ]
    return lax.ppermute(value, ("phase", "tensor"), pairs)


def add_products(source_ref, gain_ref, chunks, weights, total, squares, fresh):
    for j, chunk in enumerate(chunks):
        wide = chunk[...].astype(jnp.float32)
        gain = gain_ref[pl.ds(source_ref[j], 1), :]
        scaled = (wide * gain).astype(jnp.bfloat16)
        square = jnp.sum(wide * wide, axis=1, keepdims=True)
        held = pl.ds(pl.multiple_of(source_ref[j] * CHUNK, CHUNK), CHUNK)
        begin = 0
        for weight in weights:
            columns = slice(begin, begin + weight.shape[1])
            begin = columns.stop
            term = jnp.dot(scaled, weight[held, :], preferred_element_type=jnp.float32)
            if fresh and j == 0:
                total[:, columns] = term
            else:
                total[:, columns] += term
        if fresh and j == 0:
            squares[...] = jnp.broadcast_to(square, squares.shape)
        else:
            squares[...] += square


def first_kernel(source_ref, gain_ref, *refs):
    count = len(refs) - 5
    chunks, weights, total, squares = refs[:count], refs[count:count + 3], refs[-2], refs[-1]
    add_products(source_ref, gain_ref, chunks, weights, total, squares, True)


def heads_kernel(source_ref, first_ref, gain_ref, cos_ref, sin_ref, begun_ref, squares_ref, *refs):
    count = len(refs) - 6
    chunks, weights, out_ref, total, squares = (
        refs[:count], refs[count:count + 3], refs[-3], refs[-2], refs[-1]
    )
    rows = out_ref.shape[0]
    total[...] = begun_ref[...]
    squares[...] = squares_ref[...]
    add_products(source_ref, gain_ref, chunks, weights, total, squares, False)
    scale = lax.rsqrt(squares[...] / D + epsilon)
    cosine = cos_ref[...]
    sine = sin_ref[...]

    def turned(part):
        part = part * scale
        return (part * cosine + pltpu.roll(part, HD // 2, 1) * sine).astype(jnp.bfloat16)

    queries = [turned(total[:, i * HD:(i + 1) * HD]) for i in range(QF // HD)]
    keys = turned(total[:, QF:QF + KF])
    values = (total[:, QF + KF:] * scale).astype(jnp.bfloat16)
    heads = QF // HD
    row = lax.broadcasted_iota(jnp.int32, (heads * ROWS, ROWS), 0) % ROWS
    column = lax.broadcasted_iota(jnp.int32, (heads * ROWS, ROWS), 1)
    for m in range(rows // ROWS):
        own = slice(m * ROWS, (m + 1) * ROWS)
        first = first_ref[m]
        query = jnp.concatenate([q[own] for q in queries], axis=0)
        scores = lax.dot_general(
            query, keys[own], (((1,), (1,)), ((), ())), preferred_element_type=jnp.float32
        ) / math.sqrt(HD)
        allowed = (column <= row) & ((row < first) | (column >= first))
        scores = jnp.where(allowed, scores, -1e30)
        weights_of = jnp.exp(scores - jnp.max(scores, axis=1, keepdims=True))
        shares = (weights_of / jnp.sum(weights_of, axis=1, keepdims=True)).astype(jnp.bfloat16)
        mixed = jnp.dot(shares, values[own], preferred_element_type=jnp.float32).astype(jnp.bfloat16)
        for i in range(heads):
            out_ref[own, i * HD:(i + 1) * HD] = mixed[i * ROWS:(i + 1) * ROWS]


VMEM = pl.BlockSpec(memory_space=pltpu.VMEM)
SMEM = pl.BlockSpec(memory_space=pltpu.SMEM)
WIDE = QF + 2 * KF


def first_call(source, gain, chunks, weights):
    rows = chunks[0].shape[0]
    return pl.pallas_call(
        first_kernel,
        out_shape=[
            jax.ShapeDtypeStruct((rows, WIDE), jnp.float32),
            jax.ShapeDtypeStruct((rows, HD), jnp.float32),
        ],
        in_specs=[SMEM] + [VMEM] * (1 + len(chunks) + 3),
        out_specs=[VMEM] * 2,
        compiler_params=pltpu.CompilerParams(vmem_limit_bytes=8 * 2**20),
        cost_estimate=pl.CostEstimate(
            flops=2 * rows * len(chunks) * CHUNK * WIDE,
            bytes_accessed=2 * len(chunks) * CHUNK * WIDE, transcendentals=0
        ),
        name="first",
    )(source, gain, *chunks, *weights)


def heads_call(source, first, gain, cosine, sine, begun, squares, chunks, weights):
    rows = chunks[0].shape[0]
    return pl.pallas_call(
        heads_kernel,
        out_shape=jax.ShapeDtypeStruct((rows, QF), jnp.bfloat16),
        in_specs=[SMEM, SMEM] + [VMEM] * (5 + len(chunks) + 3),
        out_specs=VMEM,
        scratch_shapes=[
            pltpu.VMEM((rows, WIDE), jnp.float32),
            pltpu.VMEM((rows, HD), jnp.float32),
        ],
        compiler_params=pltpu.CompilerParams(vmem_limit_bytes=8 * 2**20),
        cost_estimate=pl.CostEstimate(
            flops=2 * rows * len(chunks) * CHUNK * WIDE,
            bytes_accessed=2 * len(chunks) * CHUNK * WIDE, transcendentals=0
        ),
        name="heads",
    )(source, first, gain, cosine, sine, begun, squares, *chunks, *weights)


def terms_kernel(target_ref, heads_ref, weight, *outs):
    for j, out in enumerate(outs):
        held = pl.ds(pl.multiple_of(target_ref[j] * CHUNK, CHUNK), CHUNK)
        out[...] = jnp.dot(
            heads_ref[...], weight[:, held], preferred_element_type=jnp.float32
        ).astype(jnp.bfloat16)


def terms_call(target, heads_out, weight):
    rows = heads_out.shape[0]
    count = target.shape[0]
    return pl.pallas_call(
        terms_kernel,
        out_shape=[jax.ShapeDtypeStruct((rows, CHUNK), jnp.bfloat16)] * count,
        in_specs=[SMEM, VMEM, VMEM],
        out_specs=[VMEM] * count,
        compiler_params=pltpu.CompilerParams(vmem_limit_bytes=8 * 2**20),
        cost_estimate=pl.CostEstimate(
            flops=2 * rows * QF * CHUNK * count, bytes_accessed=2 * QF * CHUNK * count, transcendentals=0
        ),
        name="terms",
    )(target, heads_out, weight)


def places(seq_parts):
    first = jnp.sum(seq_parts[:, 0, :3], axis=1)
    row = jnp.arange(ROWS, dtype=jnp.int32)[None, :]
    position = jnp.where(row < first[:, None], row, row - first[:, None]).reshape(-1)
    half = HD // 2
    frequency = jnp.exp(
        jnp.arange(half, dtype=jnp.float32) * (-2.0 * math.log(theta_base) / HD)
    )
    angles = position.astype(jnp.float32)[:, None] * frequency[None, :]
    cosine, sine = jnp.cos(angles), jnp.sin(angles)
    return (
        first,
        jnp.concatenate([cosine, cosine], axis=1),
        jnp.concatenate([-sine, sine], axis=1),
    )


def plus(one, other):
    return (one.astype(jnp.float32) + other.astype(jnp.float32)).astype(jnp.bfloat16)


def on_device(inputs, seq_parts, norm_gain, w_query, w_key, w_value, w_out):
    phase_count = lax.axis_size("phase")
    phase_index = lax.axis_index("phase")
    me = lax.axis_index("tensor")
    x, y = me // 2, me % 2

    def peers(steps, sign, row):
        return jnp.stack([((x + sign * step) % 4) * 2 + row for step in steps]).astype(jnp.int32)

    near_source, far_source = peers(GATHERED, -1, y), peers(GATHERED, -1, 1 - y)
    near_target, far_target = peers(REDUCED, 1, y), peers(REDUCED, 1, 1 - y)
    first, cosine, sine = places(seq_parts)
    gain = norm_gain.reshape(PEERS, CHUNK)
    weights, out_weight = (w_query[0], w_key[0], w_value[0]), w_out[0]
    own = inputs.reshape(MICRO * ROWS, CHUNK)
    result = jnp.zeros_like(own)
    for phase in range(phase_count):
        stay = [(p, p) for p in ((1, 3) if phase % 2 else (phase,))]
        hops = [(p - 1, p) for p in ((1, 3) if phase % 2 else (phase,))]
        if phase == 0:
            far = [moved(own, 0, 1, stay)]
            near = [own] + [moved(own, step, 0, stay) for step in GATHERED[1:]]
        else:
            far = [moved(own, 0, 1, hops)]
            near = [moved(own, step, 0, hops) for step in GATHERED]
        far += [moved(chunk, 0, 1, stay) for chunk in near[1:]]
        begun, squares = first_call(near_source, gain, near, weights)
        heads_out = heads_call(
            far_source, first, gain, cosine, sine, begun, squares, far, weights
        )
        far_terms = terms_call(far_target, heads_out, out_weight)
        arrived = [moved(term, 0, 1, stay) for term in far_terms]
        near_terms = terms_call(near_target, heads_out, out_weight)
        sums = [plus(term, other) for term, other in zip(near_terms, arrived)]
        total = near[0].astype(jnp.float32) + sums[-1].astype(jnp.float32)
        for part, step in zip(sums[:-1], REDUCED[:-1]):
            total = total + moved(part, step, 0, stay).astype(jnp.float32)
        own = total.astype(jnp.bfloat16)
        result = jnp.where(phase_index == phase, own, result)
    return result.reshape(1, MICRO, ROWS, CHUNK)


def solution(mesh):
    placed = (
        P(None, "dp", "tensor"),
        P(None, "dp", None),
        P("phase", None),
        P("phase", None, "tensor"),
        P("phase", None, "tensor"),
        P("phase", None, "tensor"),
        P("phase", "tensor", None),
    )
    return jax.shard_map(
        on_device,
        mesh=mesh,
        in_specs=placed,
        out_specs=P("phase", None, "dp", "tensor"),
        check_vma=False,
    )
```

```python
import math

import jax
import jax.numpy as jnp
from jax import lax
from jax.experimental import pallas as pl
from jax.experimental.pallas import tpu as pltpu
from jax.sharding import PartitionSpec as P

D = 8192
HD = 128
QF = 512
KF = 128
ROWS = 64
CHUNK = 1024
MICRO = 4
PEERS = 8
epsilon = 1e-05
theta_base = 10000.0

def moved(value, step, cross, hops):
    pairs = [
        (start * PEERS + x * 2 + y, end * PEERS + ((x + step) % 4) * 2 + (y ^ cross))
        for start, end in hops for x in range(4) for y in range(2)
    ]
    return lax.ppermute(value, ("phase", "tensor"), pairs)


def add_products(source_ref, gain_ref, chunks, weights, total, squares, fresh):
    rows = total.shape[0]
    parts = [(chunk, k) for chunk in chunks for k in range(chunk.shape[0] // rows)]
    for j, (chunk, k) in enumerate(parts):
        wide = chunk[k * rows:(k + 1) * rows, :].astype(jnp.float32)
        gain = gain_ref[pl.ds(source_ref[j], 1), :]
        scaled = (wide * gain).astype(jnp.bfloat16)
        square = jnp.sum(wide * wide, axis=1, keepdims=True)
        held = pl.ds(pl.multiple_of(source_ref[j] * CHUNK, CHUNK), CHUNK)
        begin = 0
        for weight in weights:
            columns = slice(begin, begin + weight.shape[1])
            begin = columns.stop
            term = jnp.dot(scaled, weight[held, :], preferred_element_type=jnp.float32)
            if fresh and j == 0:
                total[:, columns] = term
            else:
                total[:, columns] += term
        if fresh and j == 0:
            squares[...] = jnp.broadcast_to(square, squares.shape)
        else:
            squares[...] += square


def first_kernel(source_ref, gain_ref, *refs):
    count = len(refs) - 5
    chunks, weights, total, squares = refs[:count], refs[count:count + 3], refs[-2], refs[-1]
    add_products(source_ref, gain_ref, chunks, weights, total, squares, True)


def heads_kernel(source_ref, first_ref, gain_ref, cos_ref, sin_ref, begun_ref, squares_ref, *refs):
    count = len(refs) - 6
    chunks, weights, out_ref, total, squares = (
        refs[:count], refs[count:count + 3], refs[-3], refs[-2], refs[-1]
    )
    rows = out_ref.shape[0]
    total[...] = begun_ref[...]
    squares[...] = squares_ref[...]
    add_products(source_ref, gain_ref, chunks, weights, total, squares, False)
    scale = lax.rsqrt(squares[...] / D + epsilon)
    cosine = cos_ref[...]
    sine = sin_ref[...]

    def turned(part):
        part = part * scale
        return (part * cosine + pltpu.roll(part, HD // 2, 1) * sine).astype(jnp.bfloat16)

    queries = [turned(total[:, i * HD:(i + 1) * HD]) for i in range(QF // HD)]
    keys = turned(total[:, QF:QF + KF])
    values = (total[:, QF + KF:] * scale).astype(jnp.bfloat16)
    heads = QF // HD
    row = lax.broadcasted_iota(jnp.int32, (heads * ROWS, ROWS), 0) % ROWS
    column = lax.broadcasted_iota(jnp.int32, (heads * ROWS, ROWS), 1)
    for m in range(rows // ROWS):
        own = slice(m * ROWS, (m + 1) * ROWS)
        first = first_ref[m]
        query = jnp.concatenate([q[own] for q in queries], axis=0)
        scores = lax.dot_general(
            query, keys[own], (((1,), (1,)), ((), ())), preferred_element_type=jnp.float32
        ) / math.sqrt(HD)
        allowed = (column <= row) & ((row < first) | (column >= first))
        scores = jnp.where(allowed, scores, -1e30)
        weights_of = jnp.exp(scores - jnp.max(scores, axis=1, keepdims=True))
        shares = (weights_of / jnp.sum(weights_of, axis=1, keepdims=True)).astype(jnp.bfloat16)
        mixed = jnp.dot(shares, values[own], preferred_element_type=jnp.float32).astype(jnp.bfloat16)
        for i in range(heads):
            out_ref[own, i * HD:(i + 1) * HD] = mixed[i * ROWS:(i + 1) * ROWS]


VMEM = pl.BlockSpec(memory_space=pltpu.VMEM)
SMEM = pl.BlockSpec(memory_space=pltpu.SMEM)
WIDE = QF + 2 * KF


def first_call(source, gain, chunks, weights):
    rows = chunks[0].shape[0]
    return pl.pallas_call(
        first_kernel,
        out_shape=[
            jax.ShapeDtypeStruct((rows, WIDE), jnp.float32),
            jax.ShapeDtypeStruct((rows, HD), jnp.float32),
        ],
        in_specs=[SMEM] + [VMEM] * (1 + len(chunks) + 3),
        out_specs=[VMEM] * 2,
        compiler_params=pltpu.CompilerParams(vmem_limit_bytes=8 * 2**20),
        cost_estimate=pl.CostEstimate(
            flops=2 * rows * source.shape[0] * CHUNK * WIDE,
            bytes_accessed=2 * source.shape[0] * CHUNK * WIDE, transcendentals=0
        ),
        name="first",
    )(source, gain, *chunks, *weights)


def heads_call(source, first, gain, cosine, sine, begun, squares, chunks, weights):
    rows = begun.shape[0]
    return pl.pallas_call(
        heads_kernel,
        out_shape=jax.ShapeDtypeStruct((rows, QF), jnp.bfloat16),
        in_specs=[SMEM, SMEM] + [VMEM] * (5 + len(chunks) + 3),
        out_specs=VMEM,
        scratch_shapes=[
            pltpu.VMEM((rows, WIDE), jnp.float32),
            pltpu.VMEM((rows, HD), jnp.float32),
        ],
        compiler_params=pltpu.CompilerParams(vmem_limit_bytes=8 * 2**20),
        cost_estimate=pl.CostEstimate(
            flops=2 * rows * source.shape[0] * CHUNK * WIDE,
            bytes_accessed=2 * source.shape[0] * CHUNK * WIDE, transcendentals=0
        ),
        name="heads",
    )(source, first, gain, cosine, sine, begun, squares, *chunks, *weights)


def terms_kernel(target_ref, heads_ref, weight, *outs):
    rows = heads_ref.shape[0]
    parts = [(out, k) for out in outs for k in range(out.shape[0] // rows)]
    for j, (out, k) in enumerate(parts):
        held = pl.ds(pl.multiple_of(target_ref[j] * CHUNK, CHUNK), CHUNK)
        out[k * rows:(k + 1) * rows, :] = jnp.dot(
            heads_ref[...], weight[:, held], preferred_element_type=jnp.float32
        ).astype(jnp.bfloat16)


def terms_call(target, sizes, heads_out, weight):
    rows = heads_out.shape[0]
    count = target.shape[0]
    return pl.pallas_call(
        terms_kernel,
        out_shape=[jax.ShapeDtypeStruct((size * rows, CHUNK), jnp.bfloat16) for size in sizes],
        in_specs=[SMEM, VMEM, VMEM],
        out_specs=[VMEM] * len(sizes),
        compiler_params=pltpu.CompilerParams(vmem_limit_bytes=8 * 2**20),
        cost_estimate=pl.CostEstimate(
            flops=2 * rows * QF * CHUNK * count, bytes_accessed=2 * QF * CHUNK * count, transcendentals=0
        ),
        name="terms",
    )(target, heads_out, weight)


def places(seq_parts):
    first = jnp.sum(seq_parts[:, 0, :3], axis=1)
    row = jnp.arange(ROWS, dtype=jnp.int32)[None, :]
    position = jnp.where(row < first[:, None], row, row - first[:, None]).reshape(-1)
    half = HD // 2
    frequency = jnp.exp(
        jnp.arange(half, dtype=jnp.float32) * (-2.0 * math.log(theta_base) / HD)
    )
    angles = position.astype(jnp.float32)[:, None] * frequency[None, :]
    cosine, sine = jnp.cos(angles), jnp.sin(angles)
    return (
        first,
        jnp.concatenate([cosine, cosine], axis=1),
        jnp.concatenate([-sine, sine], axis=1),
    )


def added(*parts):
    total = parts[0].astype(jnp.float32)
    for part in parts[1:]:
        total = total + part.astype(jnp.float32)
    return total.astype(jnp.bfloat16)


def on_device(inputs, seq_parts, norm_gain, w_query, w_key, w_value, w_out):
    phase_count = lax.axis_size("phase")
    phase_index = lax.axis_index("phase")
    me = lax.axis_index("tensor")
    x, y = me // 2, me % 2

    def peers(*steps):
        return jnp.stack([(x + dx) % 4 * 2 + (y + dy) % 2 for dx, dy in steps]).astype(jnp.int32)

    first, cosine, sine = places(seq_parts)
    gain = norm_gain.reshape(PEERS, CHUNK)
    weights, out_weight = (w_query[0], w_key[0], w_value[0]), w_out[0]
    rows = MICRO * ROWS
    own = inputs.reshape(rows, CHUNK)
    result = jnp.zeros_like(own)
    for phase in range(phase_count):
        stay = [(p, p) for p in ((1, 3) if phase % 2 else (phase,))]
        hops = [(p - 1, p) for p in ((1, 3) if phase % 2 else (phase,))] if phase else stay
        cross = moved(own, 0, 1, hops)
        ahead, behind = moved(own, 1, 0, hops), moved(own, 3, 0, hops)
        if phase:
            own = moved(own, 0, 0, hops)
        cross_ahead, cross_behind = moved(ahead, 0, 1, stay), moved(behind, 0, 1, stay)
        opposite = moved(jnp.concatenate([own, cross], axis=0), 2, 0, stay)
        begun, squares = first_call(
            peers((0, 0), (0, 1), (3, 0), (1, 0)), gain, [own, cross, ahead, behind], weights
        )
        heads_out = heads_call(
            peers((3, 1), (1, 1), (2, 0), (2, 1)), first, gain, cosine, sine, begun, squares,
            [cross_ahead, cross_behind, opposite], weights
        )
        far_ahead, far_behind, pair = terms_call(
            peers((1, 1), (3, 1), (2, 0), (2, 1)), (1, 1, 2), heads_out, out_weight
        )
        near_ahead, near_behind, near, far = terms_call(
            peers((1, 0), (3, 0), (0, 0), (0, 1)), (1, 1, 1, 1), heads_out, out_weight
        )
        far_ahead, pair, far_behind = (
            moved(far_ahead, 0, 1, stay), moved(pair, 2, 0, stay), moved(far_behind, 0, 1, stay)
        )
        from_behind = moved(added(near_ahead, far_ahead), 1, 0, stay)
        from_ahead = moved(added(near_behind, far_behind), 3, 0, stay)
        far = moved(added(far, pair[rows:]), 0, 1, stay)
        own = added(own, near, pair[:rows], from_behind, from_ahead, far)
        result = jnp.where(phase_index == phase, own, result)
    return result.reshape(1, MICRO, ROWS, CHUNK)


def solution(mesh):
    placed = (
        P(None, "dp", "tensor"),
        P(None, "dp", None),
        P("phase", None),
        P("phase", None, "tensor"),
        P("phase", None, "tensor"),
        P("phase", None, "tensor"),
        P("phase", "tensor", None),
    )
    return jax.shard_map(
        on_device,
        mesh=mesh,
        in_specs=placed,
        out_specs=P("phase", None, "dp", "tensor"),
        check_vma=False,
    )
```

```python
import math

import jax
import jax.numpy as jnp
from jax import lax
from jax.experimental import pallas as pl
from jax.experimental.pallas import tpu as pltpu
from jax.sharding import PartitionSpec as P

D = 8192
HD = 128
QF = 512
KF = 128
ROWS = 64
CHUNK = 1024
MICRO = 4
PEERS = 8
epsilon = 1e-05
theta_base = 10000.0

def moved(value, dx, dy, hops):
    pairs = [
        (start * PEERS + x * 2 + y, end * PEERS + (x + dx) % 4 * 2 + (y + dy) % 2)
        for start, end in hops for x in range(4) for y in range(2)
    ]
    return lax.ppermute(value, ("phase", "tensor"), pairs)


def add_products(source_ref, gain_ref, chunks, weights, total, squares, fresh):
    rows = total.shape[0]
    parts = [(chunk, k) for chunk in chunks for k in range(chunk.shape[0] // rows)]
    for j, (chunk, k) in enumerate(parts):
        wide = chunk[k * rows:(k + 1) * rows, :].astype(jnp.float32)
        gain = gain_ref[pl.ds(source_ref[j], 1), :]
        scaled = (wide * gain).astype(jnp.bfloat16)
        square = jnp.sum(wide * wide, axis=1, keepdims=True)
        held = pl.ds(pl.multiple_of(source_ref[j] * CHUNK, CHUNK), CHUNK)
        begin = 0
        for weight in weights:
            columns = slice(begin, begin + weight.shape[1])
            begin = columns.stop
            term = jnp.dot(scaled, weight[held, :], preferred_element_type=jnp.float32)
            if fresh and j == 0:
                total[:, columns] = term
            else:
                total[:, columns] += term
        if fresh and j == 0:
            squares[...] = jnp.broadcast_to(square, squares.shape)
        else:
            squares[...] += square


def first_kernel(source_ref, gain_ref, *refs):
    count = len(refs) - 5
    chunks, weights, total, squares = refs[:count], refs[count:count + 3], refs[-2], refs[-1]
    add_products(source_ref, gain_ref, chunks, weights, total, squares, True)


def heads_kernel(source_ref, first_ref, gain_ref, cos_ref, sin_ref, begun_ref, squares_ref, *refs):
    count = len(refs) - 6
    chunks, weights, out_ref, total, squares = (
        refs[:count], refs[count:count + 3], refs[-3], refs[-2], refs[-1]
    )
    rows = out_ref.shape[0]
    total[...] = begun_ref[...]
    squares[...] = squares_ref[...]
    add_products(source_ref, gain_ref, chunks, weights, total, squares, False)
    scale = lax.rsqrt(squares[...] / D + epsilon)
    cosine = cos_ref[...]
    sine = sin_ref[...]

    def turned(part):
        part = part * scale
        return (part * cosine + pltpu.roll(part, HD // 2, 1) * sine).astype(jnp.bfloat16)

    queries = [turned(total[:, i * HD:(i + 1) * HD]) for i in range(QF // HD)]
    keys = turned(total[:, QF:QF + KF])
    values = (total[:, QF + KF:] * scale).astype(jnp.bfloat16)
    heads = QF // HD
    row = lax.broadcasted_iota(jnp.int32, (heads * ROWS, ROWS), 0) % ROWS
    column = lax.broadcasted_iota(jnp.int32, (heads * ROWS, ROWS), 1)
    for m in range(rows // ROWS):
        own = slice(m * ROWS, (m + 1) * ROWS)
        first = first_ref[m]
        query = jnp.concatenate([q[own] for q in queries], axis=0)
        scores = lax.dot_general(
            query, keys[own], (((1,), (1,)), ((), ())), preferred_element_type=jnp.float32
        ) / math.sqrt(HD)
        allowed = (column <= row) & ((row < first) | (column >= first))
        scores = jnp.where(allowed, scores, -1e30)
        weights_of = jnp.exp(scores - jnp.max(scores, axis=1, keepdims=True))
        shares = (weights_of / jnp.sum(weights_of, axis=1, keepdims=True)).astype(jnp.bfloat16)
        mixed = jnp.dot(shares, values[own], preferred_element_type=jnp.float32).astype(jnp.bfloat16)
        for i in range(heads):
            out_ref[own, i * HD:(i + 1) * HD] = mixed[i * ROWS:(i + 1) * ROWS]


VMEM = pl.BlockSpec(memory_space=pltpu.VMEM)
SMEM = pl.BlockSpec(memory_space=pltpu.SMEM)
WIDE = QF + 2 * KF


def first_call(source, gain, chunks, weights):
    rows = chunks[0].shape[0]
    return pl.pallas_call(
        first_kernel,
        out_shape=[
            jax.ShapeDtypeStruct((rows, WIDE), jnp.float32),
            jax.ShapeDtypeStruct((rows, HD), jnp.float32),
        ],
        in_specs=[SMEM] + [VMEM] * (1 + len(chunks) + 3),
        out_specs=[VMEM] * 2,
        compiler_params=pltpu.CompilerParams(vmem_limit_bytes=8 * 2**20),
        cost_estimate=pl.CostEstimate(
            flops=2 * rows * source.shape[0] * CHUNK * WIDE,
            bytes_accessed=2 * source.shape[0] * CHUNK * WIDE, transcendentals=0
        ),
        name="first",
    )(source, gain, *chunks, *weights)


def heads_call(source, first, gain, cosine, sine, begun, squares, chunks, weights):
    rows = begun.shape[0]
    return pl.pallas_call(
        heads_kernel,
        out_shape=jax.ShapeDtypeStruct((rows, QF), jnp.bfloat16),
        in_specs=[SMEM, SMEM] + [VMEM] * (5 + len(chunks) + 3),
        out_specs=VMEM,
        scratch_shapes=[
            pltpu.VMEM((rows, WIDE), jnp.float32),
            pltpu.VMEM((rows, HD), jnp.float32),
        ],
        compiler_params=pltpu.CompilerParams(vmem_limit_bytes=8 * 2**20),
        cost_estimate=pl.CostEstimate(
            flops=2 * rows * source.shape[0] * CHUNK * WIDE,
            bytes_accessed=2 * source.shape[0] * CHUNK * WIDE, transcendentals=0
        ),
        name="heads",
    )(source, first, gain, cosine, sine, begun, squares, *chunks, *weights)


def terms_kernel(target_ref, heads_ref, weight, *outs):
    rows = heads_ref.shape[0]
    parts = [(out, k) for out in outs for k in range(out.shape[0] // rows)]
    for j, (out, k) in enumerate(parts):
        held = pl.ds(pl.multiple_of(target_ref[j] * CHUNK, CHUNK), CHUNK)
        out[k * rows:(k + 1) * rows, :] = jnp.dot(
            heads_ref[...], weight[:, held], preferred_element_type=jnp.float32
        ).astype(jnp.bfloat16)


def terms_call(target, sizes, heads_out, weight):
    rows = heads_out.shape[0]
    count = target.shape[0]
    return pl.pallas_call(
        terms_kernel,
        out_shape=[jax.ShapeDtypeStruct((size * rows, CHUNK), jnp.bfloat16) for size in sizes],
        in_specs=[SMEM, VMEM, VMEM],
        out_specs=[VMEM] * len(sizes),
        compiler_params=pltpu.CompilerParams(vmem_limit_bytes=8 * 2**20),
        cost_estimate=pl.CostEstimate(
            flops=2 * rows * QF * CHUNK * count, bytes_accessed=2 * QF * CHUNK * count, transcendentals=0
        ),
        name="terms",
    )(target, heads_out, weight)


def places(seq_parts):
    first = jnp.sum(seq_parts[:, 0, :3], axis=1)
    row = jnp.arange(ROWS, dtype=jnp.int32)[None, :]
    position = jnp.where(row < first[:, None], row, row - first[:, None]).reshape(-1)
    half = HD // 2
    frequency = jnp.exp(
        jnp.arange(half, dtype=jnp.float32) * (-2.0 * math.log(theta_base) / HD)
    )
    angles = position.astype(jnp.float32)[:, None] * frequency[None, :]
    cosine, sine = jnp.cos(angles), jnp.sin(angles)
    return (
        first,
        jnp.concatenate([cosine, cosine], axis=1),
        jnp.concatenate([-sine, sine], axis=1),
    )


def added(*parts):
    total = parts[0].astype(jnp.float32)
    for part in parts[1:]:
        total = total + part.astype(jnp.float32)
    return total.astype(jnp.bfloat16)


def on_device(inputs, seq_parts, norm_gain, w_query, w_key, w_value, w_out):
    phase_count = lax.axis_size("phase")
    phase_index = lax.axis_index("phase")
    me = lax.axis_index("tensor")
    x, y = me // 2, me % 2

    def peers(*steps):
        return jnp.stack([(x + dx) % 4 * 2 + (y + dy) % 2 for dx, dy in steps]).astype(jnp.int32)

    first, cosine, sine = places(seq_parts)
    gain = norm_gain.reshape(PEERS, CHUNK)
    weights, out_weight = (w_query[0], w_key[0], w_value[0]), w_out[0]
    rows = MICRO * ROWS
    own = inputs.reshape(rows, CHUNK)
    result = jnp.zeros_like(own)
    for phase in range(phase_count):
        stay = [(p, p) for p in ((1, 3) if phase % 2 else (phase,))]
        hops = [(p - 1, p) for p in ((1, 3) if phase % 2 else (phase,))] if phase else stay
        turn = 1 if phase == 2 else 0
        cross = moved(own, 0, 1, hops)
        ahead, behind = moved(own, 1, 0, hops), moved(own, 3, turn, hops)
        if phase:
            own = moved(own, 0, 0, hops)
        opposite = moved(jnp.concatenate([own, cross], axis=0), 2, 0, stay)
        beside = moved(jnp.concatenate([ahead, behind], axis=0), 0, 1, stay)
        begun, squares = first_call(
            peers((0, 0), (0, 1), (3, 0), (1, turn)), gain, [own, cross, ahead, behind], weights
        )
        heads_out = heads_call(
            peers((3, 1), (1, 1 - turn), (2, 0), (2, 1)), first, gain, cosine, sine, begun, squares,
            [beside, opposite], weights
        )
        far_ahead, far_behind, pair = terms_call(
            peers((1, 1), (3, 1), (2, 0), (2, 1)), (1, 1, 2), heads_out, out_weight
        )
        near_ahead, near_behind, near, far = terms_call(
            peers((1, 0), (3, 0), (0, 0), (0, 1)), (1, 1, 1, 1), heads_out, out_weight
        )
        far_ahead, pair, far_behind = (
            moved(far_ahead, 0, 1, stay), moved(pair, 2, 0, stay), moved(far_behind, 0, 1, stay)
        )
        from_behind = moved(added(near_ahead, far_ahead), 1, 0, stay)
        from_ahead = moved(added(near_behind, far_behind), 3, 0, stay)
        far = moved(added(far, pair[rows:]), 0, 1, stay)
        own = added(own, near, pair[:rows], from_behind, from_ahead, far)
        result = jnp.where(phase_index == phase, own, result)
    return result.reshape(1, MICRO, ROWS, CHUNK)


def solution(mesh):
    placed = (
        P(None, "dp", "tensor"),
        P(None, "dp", None),
        P("phase", None),
        P("phase", None, "tensor"),
        P("phase", None, "tensor"),
        P("phase", None, "tensor"),
        P("phase", "tensor", None),
    )
    return jax.shard_map(
        on_device,
        mesh=mesh,
        in_specs=placed,
        out_specs=P("phase", None, "dp", "tensor"),
        check_vma=False,
    )
```

```python
import math

import jax
import jax.numpy as jnp
from jax import lax
from jax.experimental import pallas as pl
from jax.experimental.pallas import tpu as pltpu
from jax.sharding import PartitionSpec as P

D = 8192
HD = 128
QF = 512
KF = 128
ROWS = 64
CHUNK = 1024
MICRO = 4
PEERS = 8
epsilon = 1e-05
theta_base = 10000.0

def moved(value, dx, dy, hops):
    pairs = [
        (start * PEERS + x * 2 + y, end * PEERS + (x + dx) % 4 * 2 + (y + dy) % 2)
        for start, end in hops for x in range(4) for y in range(2)
    ]
    return lax.ppermute(value, ("phase", "tensor"), pairs)


def add_products(source_ref, gain_ref, chunks, weights, total, squares, fresh):
    rows = total.shape[0]
    parts = [(chunk, k) for chunk in chunks for k in range(chunk.shape[0] // rows)]
    for j, (chunk, k) in enumerate(parts):
        wide = chunk[k * rows:(k + 1) * rows, :].astype(jnp.float32)
        gain = gain_ref[pl.ds(source_ref[j], 1), :]
        scaled = (wide * gain).astype(jnp.bfloat16)
        square = jnp.sum(wide * wide, axis=1, keepdims=True)
        held = pl.ds(pl.multiple_of(source_ref[j] * CHUNK, CHUNK), CHUNK)
        begin = 0
        for weight in weights:
            columns = slice(begin, begin + weight.shape[1])
            begin = columns.stop
            term = jnp.dot(scaled, weight[held, :], preferred_element_type=jnp.float32)
            if fresh and j == 0:
                total[:, columns] = term
            else:
                total[:, columns] += term
        if fresh and j == 0:
            squares[...] = jnp.broadcast_to(square, squares.shape)
        else:
            squares[...] += square


def first_kernel(source_ref, gain_ref, *refs):
    count = len(refs) - 5
    chunks, weights, total, squares = refs[:count], refs[count:count + 3], refs[-2], refs[-1]
    add_products(source_ref, gain_ref, chunks, weights, total, squares, True)


def heads_kernel(source_ref, first_ref, gain_ref, cos_ref, sin_ref, begun_ref, squares_ref, *refs):
    count = len(refs) - 6
    chunks, weights, out_ref, total, squares = (
        refs[:count], refs[count:count + 3], refs[-3], refs[-2], refs[-1]
    )
    rows = out_ref.shape[0]
    total[...] = begun_ref[...]
    squares[...] = squares_ref[...]
    add_products(source_ref, gain_ref, chunks, weights, total, squares, False)
    scale = lax.rsqrt(squares[...] / D + epsilon)
    cosine = cos_ref[...]
    sine = sin_ref[...]

    def turned(part):
        part = part * scale
        return (part * cosine + pltpu.roll(part, HD // 2, 1) * sine).astype(jnp.bfloat16)

    queries = [turned(total[:, i * HD:(i + 1) * HD]) for i in range(QF // HD)]
    keys = turned(total[:, QF:QF + KF])
    values = (total[:, QF + KF:] * scale).astype(jnp.bfloat16)
    heads = QF // HD
    row = lax.broadcasted_iota(jnp.int32, (heads * ROWS, ROWS), 0) % ROWS
    column = lax.broadcasted_iota(jnp.int32, (heads * ROWS, ROWS), 1)
    for m in range(rows // ROWS):
        own = slice(m * ROWS, (m + 1) * ROWS)
        first = first_ref[m]
        query = jnp.concatenate([q[own] for q in queries], axis=0)
        scores = lax.dot_general(
            query, keys[own], (((1,), (1,)), ((), ())), preferred_element_type=jnp.float32
        ) / math.sqrt(HD)
        allowed = (column <= row) & ((row < first) | (column >= first))
        scores = jnp.where(allowed, scores, -1e30)
        weights_of = jnp.exp(scores - jnp.max(scores, axis=1, keepdims=True))
        shares = (weights_of / jnp.sum(weights_of, axis=1, keepdims=True)).astype(jnp.bfloat16)
        mixed = jnp.dot(shares, values[own], preferred_element_type=jnp.float32).astype(jnp.bfloat16)
        for i in range(heads):
            out_ref[own, i * HD:(i + 1) * HD] = mixed[i * ROWS:(i + 1) * ROWS]


VMEM = pl.BlockSpec(memory_space=pltpu.VMEM)
SMEM = pl.BlockSpec(memory_space=pltpu.SMEM)
WIDE = QF + 2 * KF


def first_call(source, gain, chunks, weights):
    rows = chunks[0].shape[0]
    return pl.pallas_call(
        first_kernel,
        out_shape=[
            jax.ShapeDtypeStruct((rows, WIDE), jnp.float32),
            jax.ShapeDtypeStruct((rows, HD), jnp.float32),
        ],
        in_specs=[SMEM] + [VMEM] * (1 + len(chunks) + 3),
        out_specs=[VMEM] * 2,
        compiler_params=pltpu.CompilerParams(vmem_limit_bytes=8 * 2**20),
        cost_estimate=pl.CostEstimate(
            flops=2 * rows * source.shape[0] * CHUNK * WIDE,
            bytes_accessed=2 * source.shape[0] * CHUNK * WIDE, transcendentals=0
        ),
        name="first",
    )(source, gain, *chunks, *weights)


def heads_call(source, first, gain, cosine, sine, begun, squares, chunks, weights):
    rows = begun.shape[0]
    return pl.pallas_call(
        heads_kernel,
        out_shape=jax.ShapeDtypeStruct((rows, QF), jnp.bfloat16),
        in_specs=[SMEM, SMEM] + [VMEM] * (5 + len(chunks) + 3),
        out_specs=VMEM,
        scratch_shapes=[
            pltpu.VMEM((rows, WIDE), jnp.float32),
            pltpu.VMEM((rows, HD), jnp.float32),
        ],
        compiler_params=pltpu.CompilerParams(vmem_limit_bytes=8 * 2**20),
        cost_estimate=pl.CostEstimate(
            flops=2 * rows * source.shape[0] * CHUNK * WIDE,
            bytes_accessed=2 * source.shape[0] * CHUNK * WIDE, transcendentals=0
        ),
        name="heads",
    )(source, first, gain, cosine, sine, begun, squares, *chunks, *weights)


def terms_kernel(target_ref, heads_ref, weight, *outs):
    rows = heads_ref.shape[0]
    parts = [(out, k) for out in outs for k in range(out.shape[0] // rows)]
    for j, (out, k) in enumerate(parts):
        held = pl.ds(pl.multiple_of(target_ref[j] * CHUNK, CHUNK), CHUNK)
        out[k * rows:(k + 1) * rows, :] = jnp.dot(
            heads_ref[...], weight[:, held], preferred_element_type=jnp.float32
        ).astype(jnp.bfloat16)


def terms_call(target, sizes, heads_out, weight):
    rows = heads_out.shape[0]
    count = target.shape[0]
    return pl.pallas_call(
        terms_kernel,
        out_shape=[jax.ShapeDtypeStruct((size * rows, CHUNK), jnp.bfloat16) for size in sizes],
        in_specs=[SMEM, VMEM, VMEM],
        out_specs=[VMEM] * len(sizes),
        compiler_params=pltpu.CompilerParams(vmem_limit_bytes=8 * 2**20),
        cost_estimate=pl.CostEstimate(
            flops=2 * rows * QF * CHUNK * count, bytes_accessed=2 * QF * CHUNK * count, transcendentals=0
        ),
        name="terms",
    )(target, heads_out, weight)


def places(seq_parts):
    first = jnp.sum(seq_parts[:, 0, :3], axis=1)
    row = jnp.arange(ROWS, dtype=jnp.int32)[None, :]
    position = jnp.where(row < first[:, None], row, row - first[:, None]).reshape(-1)
    half = HD // 2
    frequency = jnp.exp(
        jnp.arange(half, dtype=jnp.float32) * (-2.0 * math.log(theta_base) / HD)
    )
    angles = position.astype(jnp.float32)[:, None] * frequency[None, :]
    cosine, sine = jnp.cos(angles), jnp.sin(angles)
    return (
        first,
        jnp.concatenate([cosine, cosine], axis=1),
        jnp.concatenate([-sine, sine], axis=1),
    )


def added(*parts):
    total = parts[0].astype(jnp.float32)
    for part in parts[1:]:
        total = total + part.astype(jnp.float32)
    return total.astype(jnp.bfloat16)


def on_device(inputs, seq_parts, norm_gain, w_query, w_key, w_value, w_out):
    phase_count = lax.axis_size("phase")
    phase_index = lax.axis_index("phase")
    me = lax.axis_index("tensor")
    x, y = me // 2, me % 2

    def peers(*steps):
        return jnp.stack([(x + dx) % 4 * 2 + (y + dy) % 2 for dx, dy in steps]).astype(jnp.int32)

    first, cosine, sine = places(seq_parts)
    gain = norm_gain.reshape(PEERS, CHUNK)
    weights, out_weight = (w_query[0], w_key[0], w_value[0]), w_out[0]
    rows = MICRO * ROWS
    own = inputs.reshape(rows, CHUNK)
    result = jnp.zeros_like(own)
    for phase in range(phase_count):
        stay = [(p, p) for p in ((1, 3) if phase % 2 else (phase,))]
        hops = [(p - 1, p) for p in ((1, 3) if phase % 2 else (phase,))] if phase else [(1, 0)]
        turn = 1 if phase == 2 else 0
        cross = moved(own, 0, 1, hops)
        ahead, behind = moved(own, 1, 0, hops), moved(own, 3, turn, hops)
        if phase:
            own = moved(own, 0, 0, hops)
        opposite = moved(jnp.concatenate([own, cross], axis=0), 2, 0, stay)
        beside = moved(jnp.concatenate([ahead, behind], axis=0), 0, 1, stay)
        begun, squares = first_call(
            peers((0, 0), (0, 1), (3, 0), (1, turn)), gain, [own, cross, ahead, behind], weights
        )
        heads_out = heads_call(
            peers((3, 1), (1, 1 - turn), (2, 0), (2, 1)), first, gain, cosine, sine, begun, squares,
            [beside, opposite], weights
        )
        pair, far_ahead, far_behind = terms_call(
            peers((2, 0), (2, 1), (1, 1), (3, 1)), (2, 1, 1), heads_out, out_weight
        )
        far, near_ahead, near_behind, near = terms_call(
            peers((0, 1), (1, 0), (3, 0), (0, 0)), (1, 1, 1, 1), heads_out, out_weight
        )
        pair = moved(pair, 2, 0, stay)
        far = moved(added(far, pair[rows:]), 0, 1, stay)
        far_ahead, far_behind = moved(far_ahead, 0, 1, stay), moved(far_behind, 0, 1, stay)
        from_behind = moved(added(near_ahead, far_ahead), 1, 0, stay)
        from_ahead = moved(added(near_behind, far_behind), 3, 0, stay)
        own = added(far, own, near, pair[:rows], from_behind, from_ahead)
        result = jnp.where(phase_index == phase, own, result)
    return result.reshape(1, MICRO, ROWS, CHUNK)


def solution(mesh):
    placed = (
        P(None, "dp", "tensor"),
        P(None, "dp", None),
        P("phase", None),
        P("phase", None, "tensor"),
        P("phase", None, "tensor"),
        P("phase", None, "tensor"),
        P("phase", "tensor", None),
    )
    return jax.shard_map(
        on_device,
        mesh=mesh,
        in_specs=placed,
        out_specs=P("phase", None, "dp", "tensor"),
        check_vma=False,
    )
```

```python
import math

import jax
import jax.numpy as jnp
from jax import lax
from jax.experimental import pallas as pl
from jax.experimental.pallas import tpu as pltpu
from jax.sharding import PartitionSpec as P

D = 8192
HD = 128
QF = 512
KF = 128
ROWS = 64
CHUNK = 1024
MICRO = 4
PEERS = 8
epsilon = 1e-05
theta_base = 10000.0

def moved(value, dx, dy, hops):
    pairs = [
        (start * PEERS + x * 2 + y, end * PEERS + (x + dx) % 4 * 2 + (y + dy) % 2)
        for start, end in hops for x in range(4) for y in range(2)
    ]
    return lax.ppermute(value, ("phase", "tensor"), pairs)


def add_products(source_ref, gain_ref, chunks, weights, total, squares, fresh):
    rows = total.shape[0]
    parts = [(chunk, k) for chunk in chunks for k in range(chunk.shape[0] // rows)]
    for j, (chunk, k) in enumerate(parts):
        wide = chunk[k * rows:(k + 1) * rows, :].astype(jnp.float32)
        gain = gain_ref[pl.ds(source_ref[j], 1), :]
        scaled = (wide * gain).astype(jnp.bfloat16)
        square = jnp.sum(wide * wide, axis=1, keepdims=True)
        held = pl.ds(pl.multiple_of(source_ref[j] * CHUNK, CHUNK), CHUNK)
        begin = 0
        for weight in weights:
            columns = slice(begin, begin + weight.shape[1])
            begin = columns.stop
            term = jnp.dot(scaled, weight[held, :], preferred_element_type=jnp.float32)
            if fresh and j == 0:
                total[:, columns] = term
            else:
                total[:, columns] += term
        if fresh and j == 0:
            squares[...] = jnp.broadcast_to(square, squares.shape)
        else:
            squares[...] += square


def first_kernel(source_ref, gain_ref, *refs):
    count = len(refs) - 5
    chunks, weights, total, squares = refs[:count], refs[count:count + 3], refs[-2], refs[-1]
    add_products(source_ref, gain_ref, chunks, weights, total, squares, True)


def heads_kernel(source_ref, first_ref, gain_ref, cos_ref, sin_ref, begun_ref, squares_ref, *refs):
    count = len(refs) - 6
    chunks, weights, out_ref, total, squares = (
        refs[:count], refs[count:count + 3], refs[-3], refs[-2], refs[-1]
    )
    rows = out_ref.shape[0]
    total[...] = begun_ref[...]
    squares[...] = squares_ref[...]
    add_products(source_ref, gain_ref, chunks, weights, total, squares, False)
    scale = lax.rsqrt(squares[...] / D + epsilon)
    cosine = cos_ref[...]
    sine = sin_ref[...]

    def turned(part):
        part = part * scale
        return (part * cosine + pltpu.roll(part, HD // 2, 1) * sine).astype(jnp.bfloat16)

    queries = [turned(total[:, i * HD:(i + 1) * HD]) for i in range(QF // HD)]
    keys = turned(total[:, QF:QF + KF])
    values = (total[:, QF + KF:] * scale).astype(jnp.bfloat16)
    heads = QF // HD
    row = lax.broadcasted_iota(jnp.int32, (heads * ROWS, ROWS), 0) % ROWS
    column = lax.broadcasted_iota(jnp.int32, (heads * ROWS, ROWS), 1)
    for m in range(rows // ROWS):
        own = slice(m * ROWS, (m + 1) * ROWS)
        first = first_ref[m]
        query = jnp.concatenate([q[own] for q in queries], axis=0)
        scores = lax.dot_general(
            query, keys[own], (((1,), (1,)), ((), ())), preferred_element_type=jnp.float32
        ) / math.sqrt(HD)
        allowed = (column <= row) & ((row < first) | (column >= first))
        scores = jnp.where(allowed, scores, -1e30)
        weights_of = jnp.exp(scores - jnp.max(scores, axis=1, keepdims=True))
        shares = (weights_of / jnp.sum(weights_of, axis=1, keepdims=True)).astype(jnp.bfloat16)
        mixed = jnp.dot(shares, values[own], preferred_element_type=jnp.float32).astype(jnp.bfloat16)
        for i in range(heads):
            out_ref[own, i * HD:(i + 1) * HD] = mixed[i * ROWS:(i + 1) * ROWS]


VMEM = pl.BlockSpec(memory_space=pltpu.VMEM)
SMEM = pl.BlockSpec(memory_space=pltpu.SMEM)
WIDE = QF + 2 * KF


def first_call(source, gain, chunks, weights):
    rows = chunks[0].shape[0]
    return pl.pallas_call(
        first_kernel,
        out_shape=[
            jax.ShapeDtypeStruct((rows, WIDE), jnp.float32),
            jax.ShapeDtypeStruct((rows, HD), jnp.float32),
        ],
        in_specs=[SMEM] + [VMEM] * (1 + len(chunks) + 3),
        out_specs=[VMEM] * 2,
        compiler_params=pltpu.CompilerParams(vmem_limit_bytes=8 * 2**20),
        cost_estimate=pl.CostEstimate(
            flops=2 * rows * source.shape[0] * CHUNK * WIDE,
            bytes_accessed=2 * source.shape[0] * CHUNK * WIDE, transcendentals=0
        ),
        name="first",
    )(source, gain, *chunks, *weights)


def heads_call(source, first, gain, cosine, sine, begun, squares, chunks, weights):
    rows = begun.shape[0]
    return pl.pallas_call(
        heads_kernel,
        out_shape=jax.ShapeDtypeStruct((rows, QF), jnp.bfloat16),
        in_specs=[SMEM, SMEM] + [VMEM] * (5 + len(chunks) + 3),
        out_specs=VMEM,
        scratch_shapes=[
            pltpu.VMEM((rows, WIDE), jnp.float32),
            pltpu.VMEM((rows, HD), jnp.float32),
        ],
        compiler_params=pltpu.CompilerParams(vmem_limit_bytes=8 * 2**20),
        cost_estimate=pl.CostEstimate(
            flops=2 * rows * source.shape[0] * CHUNK * WIDE,
            bytes_accessed=2 * source.shape[0] * CHUNK * WIDE, transcendentals=0
        ),
        name="heads",
    )(source, first, gain, cosine, sine, begun, squares, *chunks, *weights)


def terms_kernel(target_ref, heads_ref, weight, *outs):
    rows = heads_ref.shape[0]
    parts = [(out, k) for out in outs for k in range(out.shape[0] // rows)]
    for j, (out, k) in enumerate(parts):
        held = pl.ds(pl.multiple_of(target_ref[j] * CHUNK, CHUNK), CHUNK)
        out[k * rows:(k + 1) * rows, :] = jnp.dot(
            heads_ref[...], weight[:, held], preferred_element_type=jnp.float32
        ).astype(jnp.bfloat16)


def terms_call(target, sizes, heads_out, weight):
    rows = heads_out.shape[0]
    count = target.shape[0]
    return pl.pallas_call(
        terms_kernel,
        out_shape=[jax.ShapeDtypeStruct((size * rows, CHUNK), jnp.bfloat16) for size in sizes],
        in_specs=[SMEM, VMEM, VMEM],
        out_specs=[VMEM] * len(sizes),
        compiler_params=pltpu.CompilerParams(vmem_limit_bytes=8 * 2**20),
        cost_estimate=pl.CostEstimate(
            flops=2 * rows * QF * CHUNK * count, bytes_accessed=2 * QF * CHUNK * count, transcendentals=0
        ),
        name="terms",
    )(target, heads_out, weight)


def places(seq_parts):
    first = jnp.sum(seq_parts[:, 0, :3], axis=1)
    row = jnp.arange(ROWS, dtype=jnp.int32)[None, :]
    position = jnp.where(row < first[:, None], row, row - first[:, None]).reshape(-1)
    half = HD // 2
    frequency = jnp.exp(
        jnp.arange(half, dtype=jnp.float32) * (-2.0 * math.log(theta_base) / HD)
    )
    angles = position.astype(jnp.float32)[:, None] * frequency[None, :]
    cosine, sine = jnp.cos(angles), jnp.sin(angles)
    return (
        first,
        jnp.concatenate([cosine, cosine], axis=1),
        jnp.concatenate([-sine, sine], axis=1),
    )


def added(*parts):
    total = parts[0].astype(jnp.float32)
    for part in parts[1:]:
        total = total + part.astype(jnp.float32)
    return total.astype(jnp.bfloat16)


def on_device(inputs, seq_parts, norm_gain, w_query, w_key, w_value, w_out):
    phase_count = lax.axis_size("phase")
    phase_index = lax.axis_index("phase")
    me = lax.axis_index("tensor")
    x, y = me // 2, me % 2

    def peers(*steps):
        return jnp.stack([(x + dx) % 4 * 2 + (y + dy) % 2 for dx, dy in steps]).astype(jnp.int32)

    first, cosine, sine = places(seq_parts)
    gain = norm_gain.reshape(PEERS, CHUNK)
    weights, out_weight = (w_query[0], w_key[0], w_value[0]), w_out[0]
    rows = MICRO * ROWS
    own = inputs.reshape(rows, CHUNK)
    result = jnp.zeros_like(own)
    for phase in range(phase_count):
        stay = [(p, p) for p in ((1, 3) if phase % 2 else (phase,))]
        hops = [(p - 1, p) for p in ((1, 3) if phase % 2 else (phase,))] if phase else [(1, 0)]
        turn = 1 if phase == 2 else 0
        turn = 1 if phase == 2 else 0
        if phase == 0:
            far_hops = [(2, 0)]
            cross, far_ahead = moved(own, 0, 1, far_hops), moved(own, 1, 1, far_hops)
            ahead, behind = moved(own, 1, 0, hops), moved(own, 3, 0, hops)
            far_behind, far_opposite = moved(own, 3, 1, far_hops), moved(own, 2, 1, far_hops)
            last = [far_ahead, far_behind, moved(own, 2, 0, hops), far_opposite]
        else:
            cross = moved(own, 0, 1, hops)
            ahead, behind = moved(own, 1, 0, hops), moved(own, 3, turn, hops)
            if phase:
                own = moved(own, 0, 0, hops)
            opposite = moved(jnp.concatenate([own, cross], axis=0), 2, 0, stay)
            beside = moved(jnp.concatenate([ahead, behind], axis=0), 0, 1, stay)
            last = [beside, opposite]
        begun, squares = first_call(
            peers((0, 0), (0, 1), (3, 0), (1, turn)), gain, [own, cross, ahead, behind], weights
        )
        heads_out = heads_call(
            peers((3, 1), (1, 1 - turn), (2, 0), (2, 1)), first, gain, cosine, sine, begun, squares,
            last, weights
        )
        pair, far_ahead, far_behind = terms_call(
            peers((2, 0), (2, 1), (1, 1), (3, 1)), (2, 1, 1), heads_out, out_weight
        )
        far, near_ahead, near_behind, near = terms_call(
            peers((0, 1), (1, 0), (3, 0), (0, 0)), (1, 1, 1, 1), heads_out, out_weight
        )
        pair = moved(pair, 2, 0, stay)
        far = moved(added(far, pair[rows:]), 0, 1, stay)
        far_ahead, far_behind = moved(far_ahead, 0, 1, stay), moved(far_behind, 0, 1, stay)
        from_behind = moved(added(near_ahead, far_ahead), 1, 0, stay)
        from_ahead = moved(added(near_behind, far_behind), 3, 0, stay)
        own = added(far, own, near, pair[:rows], from_behind, from_ahead)
        result = jnp.where(phase_index == phase, own, result)
    return result.reshape(1, MICRO, ROWS, CHUNK)


def solution(mesh):
    placed = (
        P(None, "dp", "tensor"),
        P(None, "dp", None),
        P("phase", None),
        P("phase", None, "tensor"),
        P("phase", None, "tensor"),
        P("phase", None, "tensor"),
        P("phase", "tensor", None),
    )
    return jax.shard_map(
        on_device,
        mesh=mesh,
        in_specs=placed,
        out_specs=P("phase", None, "dp", "tensor"),
        check_vma=False,
    )
```
